32 devices in a mesh: image: 4 (over y, x), crop: 2 (over core), proto: 4 (over z).
Axes of the slice: x: 2, y: 2, z: 4, core: 2. Of those that a mesh axis runs over, the one named last changes fastest.
Arguments:
- teacher_feats: bfloat16 [256, 2, 512], P('image'), may hold values from -4 to 4
- student_feats: bfloat16 [8, 256, 512], P('crop', 'image'), may hold values from -4 to 4
- teacher_protos: bfloat16 [512, 16384], P(None, ('crop', 'proto')), may hold values from -6 to 6
- student_protos: bfloat16 [512, 16384], P(None, ('crop', 'proto')), may hold values from -6 to 6
- pairing: int32 [8, 256], P('crop', 'image'), may hold values from 0 to 1
- row_weight: bfloat16 [8, 256], P('crop', 'image'), may hold values from 0.5 to 4
Outputs:
- feat_grad: float32 [8, 256, 512], P('crop', 'image')
- row_loss: float32 [8, 256], P('crop', 'image')
The draws below stay inside these ranges and needn't reach their ends.
All inputs are finite; a program needn't handle non-finite values.
Results may differ from the reference program's by a relative error of at most 0.0016.
Values may be sent and summed in bfloat16 or wider, within the bound.
No kernel may reach another device: no remote copies, remote signals or barrier semaphores. Data moves between devices by JAX's collectives and lax.ppermute only.
A program may use at most 64 MiB of HBM per device.

```python
import math
import jax
import jax.numpy as jnp
from jax import lax

D = 512
LOCAL = 8
GLOBAL = 2
SWEEPS = 3
IMAGES = 256
PROTOS = 16384


concept_count = 32


def concept_directions(key):
    return jax.random.normal(jax.random.fold_in(key, 7001), (concept_count, D), jnp.float32)


def image_concepts(key):
    return jax.random.randint(jax.random.fold_in(key, 7002), (IMAGES, 3), 0, concept_count)


def placed_protos(key):
    sub_key = jax.random.fold_in(key, 7003)
    entries = jax.random.normal(sub_key, (D, PROTOS), jnp.float32)
    directions = concept_directions(key)
    position = jnp.arange(PROTOS, dtype=jnp.float32) / PROTOS
    member_draw = jax.random.uniform(jax.random.fold_in(key, 7005), (PROTOS,), jnp.float32, 0.0, 1.0)
    member = member_draw < 0.25 + 0.5 * position
    owner = jax.random.randint(jax.random.fold_in(key, 7006), (PROTOS,), 0, concept_count)
    cosine = jax.random.uniform(jax.random.fold_in(key, 7007), (PROTOS,), jnp.float32, 0.3, 0.9)
    centre = directions[owner].T
    clustered = cosine[None, :] * centre + jnp.sqrt(1.0 - cosine * cosine)[None, :] * entries
    return jnp.where(member[None, :], clustered, entries)


def mixed_rows(key, salt, row_count):
    directions = concept_directions(key)[image_concepts(key)] / math.sqrt(D)
    mixture = jax.random.uniform(jax.random.fold_in(key, salt), (row_count, IMAGES, 3), jnp.float32, 0.0, 1.0)
    noise_term = 0.3 * jax.random.normal(jax.random.fold_in(key, salt + 1), (row_count, IMAGES, D), jnp.float32)
    return jnp.einsum('cij,ijd->cid', mixture, directions) + noise_term / math.sqrt(D)


def draw_teacher_feats(key, part):
    samples = 3.0 * mixed_rows(key, 7010, GLOBAL)
    return jnp.clip(jnp.transpose(samples, (1, 0, 2)), -4.0, 4.0).astype(jnp.bfloat16)


def draw_student_feats(key, part):
    samples = mixed_rows(key, 7020, LOCAL)
    lowest, highest = (0.05, 0.5)
    exponent = jax.random.uniform(jax.random.fold_in(key, 7030), (LOCAL, IMAGES, 1), jnp.float32, math.log(lowest), math.log(highest))
    return jnp.clip(samples * jnp.exp(exponent), -4.0, 4.0).astype(jnp.bfloat16)


def draw_student_protos(key, part):
    return jnp.clip(placed_protos(key), -6.0, 6.0).astype(jnp.bfloat16)


def draw_teacher_protos(key, part):
    drift_term = 0.3 * jax.random.normal(jax.random.fold_in(key, 7004), (D, PROTOS), jnp.float32)
    return jnp.clip(placed_protos(key) + drift_term, -6.0, 6.0).astype(jnp.bfloat16)


def set_ends(array, rng, least, high):
    dims = array.shape
    place = [jax.random.randint(jax.random.fold_in(rng, axis), (), 0, dims[axis]) for axis in range(len(dims))]
    array = array.at[tuple(place)].set(least)
    longest = dims.index(max(dims))
    place[longest] = (place[longest] + 1) % dims[longest]
    return array.at[tuple(place)].set(high)


def shard_levels(stream_key, shape, cuts, least, high):
    def one(axis_at, shards_of):
        heights = jax.random.uniform(jax.random.fold_in(jax.random.fold_in(stream_key, 6), axis_at), (shards_of,), jnp.float32, least / len(cuts), high / len(cuts))
        return jnp.repeat(jnp.exp(heights), shape[axis_at] // shards_of).reshape((-1,) + (1,) * (len(shape) - axis_at - 1))

    gain = one(*cuts[0])
    for cut in cuts[1:]:
        gain = gain * one(*cut)
    return gain


def setup_inputs(seed: int = 0) -> dict:
    seeds = jax.random.split(jax.random.key(seed), 7)
    return {
        "teacher_feats": draw_teacher_feats(jax.random.fold_in(seeds[6], 71), 0),
        "student_feats": draw_student_feats(jax.random.fold_in(seeds[6], 71), 0),
        "teacher_protos": draw_teacher_protos(jax.random.fold_in(seeds[6], 71), 0),
        "student_protos": draw_student_protos(jax.random.fold_in(seeds[6], 71), 0),
        "pairing": set_ends(jax.random.randint(seeds[4], (LOCAL, IMAGES), 0, GLOBAL), jax.random.fold_in(seeds[4], 1), 0, GLOBAL - 1).astype(jnp.int32),
        "row_weight": jnp.clip(jnp.exp(math.log(4.0) - 2.0794415 * jax.random.uniform(seeds[5], (LOCAL, IMAGES), jnp.float32) ** shard_levels(seeds[5], (LOCAL, IMAGES), ((0, 2), (1, 4)), -0.2, 0.2)), 0.5, 4.0).astype(jnp.bfloat16),
    }


epsilon = 1e-06
student_softness = 0.1
teacher_softness = 0.04

def unit_rows(raw_rows):
    return raw_rows * lax.rsqrt(lax.optimization_barrier(jnp.sum(raw_rows * raw_rows, axis=-1, keepdims=True)) + epsilon)

def unit_columns(weight_rows):
    entries = weight_rows.astype(jnp.float32)
    return (entries * lax.rsqrt(lax.optimization_barrier(jnp.sum(entries * entries, axis=0, keepdims=True)) + epsilon)).astype(jnp.bfloat16)

def finish_rows(raw_rows, back_sum, cross_term, running_sums):
    scales = lax.rsqrt(lax.optimization_barrier(jnp.sum(raw_rows * raw_rows, axis=-1, keepdims=True)) + epsilon)
    along = lax.optimization_barrier(jnp.sum(raw_rows * back_sum, axis=-1, keepdims=True))
    gradient = scales * back_sum - scales * scales * scales * raw_rows * along
    return (gradient, jnp.log(running_sums) - cross_term)

def reference(teacher_feats, student_feats, teacher_protos, student_protos, pairing, row_weight):
    teacher_normalized_rows = unit_rows(teacher_feats.astype(jnp.float32)).astype(jnp.bfloat16).reshape(IMAGES * GLOBAL, D)
    teacher_weight_matrix = unit_columns(teacher_protos)
    student_weight_matrix = unit_columns(student_protos)
    transport_plan = jnp.exp(jnp.dot(teacher_normalized_rows, teacher_weight_matrix, preferred_element_type=jnp.float32) / teacher_softness)
    for sweep_index in range(SWEEPS):
        transport_plan = transport_plan / lax.optimization_barrier(jnp.sum(transport_plan, axis=0, keepdims=True))
        transport_plan = transport_plan / lax.optimization_barrier(jnp.sum(transport_plan, axis=1, keepdims=True))
    targets = transport_plan.astype(jnp.bfloat16).reshape(IMAGES, GLOBAL, PROTOS)

    def crop_step(inputs):
        features, picked, weight_rows = inputs
        raw_rows = features.astype(jnp.float32)
        student_normalized_rows = unit_rows(raw_rows).astype(jnp.bfloat16)
        score_matrix = jnp.dot(student_normalized_rows, student_weight_matrix, preferred_element_type=jnp.float32) / student_softness
        exponent_terms = jnp.exp(score_matrix)
        running_sums = lax.optimization_barrier(jnp.sum(exponent_terms, axis=1))
        selected_entries = jnp.zeros(score_matrix.shape, jnp.float32)
        for view_index in range(GLOBAL):
            selected_entries = jnp.where((picked == view_index)[:, None], targets[:, view_index, :].astype(jnp.float32), selected_entries)
        cross_term = lax.optimization_barrier(jnp.sum(selected_entries * score_matrix, axis=1))
        linear_factors = (weight_rows.astype(jnp.float32)[:, None] * (exponent_terms / running_sums[:, None] - selected_entries) / student_softness).astype(jnp.bfloat16)
        back_sum = jnp.dot(linear_factors, student_weight_matrix.T, preferred_element_type=jnp.float32)
        return finish_rows(raw_rows, back_sum, cross_term, running_sums)
    gradients, losses = lax.map(crop_step, (student_feats, pairing, row_weight))
    return (gradients, losses)
```

```python
import functools

import jax
import jax.numpy as jnp
from jax import lax
from jax.experimental import pallas as pl
from jax.experimental.pallas import tpu as pltpu
from jax.sharding import PartitionSpec as P

SWEEPS = 3
LANES = 128
VMEM_LIMIT = 40 * 1024 * 1024

epsilon = 1e-06
student_softness = 0.1
teacher_softness = 0.04

F32 = jnp.float32
BF16 = jnp.bfloat16


def unit_rows(raw_rows):
    return raw_rows * lax.rsqrt(jnp.sum(raw_rows * raw_rows, axis=-1, keepdims=True) + epsilon)


def unit_columns(entries):
    return entries * lax.rsqrt(jnp.sum(entries * entries, axis=0, keepdims=True) + epsilon)


def lane_groups(values):
    total = values[:, :LANES]
    for start in range(LANES, values.shape[1], LANES):
        total = total + values[:, start : start + LANES]
    return total


def dot_t(a, b):
    return lax.dot_general(a, b, (((1,), (1,)), ((), ())), preferred_element_type=F32)


def row_vector(partial):
    return jnp.sum(partial.T, axis=0, keepdims=True)


def student_kernel(*refs):
    feats, (protos, unit_protos, back, unit_feats) = refs[:-4], refs[-4:]
    width = protos.shape[0]

    @pl.when(pl.program_id(0) == 0)
    def _():
        start = 0
        for part in feats:
            rows = part.shape[0]
            unit_feats[start : start + rows, :] = unit_rows(part[...].astype(F32)).astype(BF16)
            start += rows
        back[...] = jnp.zeros_like(back)

    weights = unit_columns(protos[...].astype(F32)).astype(BF16)
    unit_protos[...] = weights
    logits = jnp.dot(unit_feats[...], weights, preferred_element_type=F32)
    terms = jnp.exp(logits * (1.0 / student_softness))
    back[:, width:] += lane_groups(terms)
    back[:, :width] += dot_t(terms.astype(BF16), weights)


def student_call(feats, protos, block):
    width, columns = protos.shape
    rows = sum(part.shape[0] for part in feats)
    return pl.pallas_call(
        student_kernel,
        grid=(columns // block,),
        in_specs=[pl.BlockSpec(part.shape, lambda i: (0, 0)) for part in feats]
        + [pl.BlockSpec((width, block), lambda i: (0, i))],
        out_specs=[
            pl.BlockSpec((width, block), lambda i: (0, i)),
            pl.BlockSpec((rows, width + LANES), lambda i: (0, 0)),
        ],
        out_shape=[
            jax.ShapeDtypeStruct((width, columns), BF16),
            jax.ShapeDtypeStruct((rows, width + LANES), F32),
        ],
        scratch_shapes=[pltpu.VMEM((rows, width), BF16)],
        compiler_params=pltpu.CompilerParams(vmem_limit_bytes=VMEM_LIMIT),
        cost_estimate=pl.CostEstimate(
            flops=4 * rows * width * columns, bytes_accessed=4 * width * columns, transcendentals=rows * columns
        ),
        name="student",
    )(*feats, protos)


def first_kernel(*refs):
    parts, (protos, plan, sums, partial) = refs[:-4], refs[-4:]

    @pl.when(pl.program_id(0) == 0)
    def _():
        partial[...] = jnp.zeros_like(partial)

    weights = unit_columns(protos[...].astype(F32)).astype(BF16)
    column_sums = None
    start = 0
    for part in parts:
        rows = part.shape[0]
        values = jnp.exp(
            jnp.dot(part[...], weights, preferred_element_type=F32) * (1.0 / teacher_softness)
        )
        plan[start : start + rows, :] = values
        here = jnp.sum(values, axis=0, keepdims=True)
        column_sums = here if column_sums is None else column_sums + here
        start += rows
    scale = 1.0 / column_sums
    partial[...] += lane_groups(plan[...] * scale)

    @pl.when(pl.program_id(0) == pl.num_programs(0) - 1)
    def _():
        sums[...] = jnp.broadcast_to(row_vector(partial[...]), sums.shape)


def first_call(parts, protos, copies, block):
    width, columns = protos.shape
    rows = sum(part.shape[0] for part in parts)
    return pl.pallas_call(
        first_kernel,
        grid=(columns // block,),
        in_specs=[pl.BlockSpec(part.shape, lambda i: (0, 0)) for part in parts]
        + [pl.BlockSpec((width, block), lambda i: (0, i))],
        out_specs=[
            pl.BlockSpec((rows, block), lambda i: (0, i)),
            pl.BlockSpec((copies, rows), lambda i: (0, 0)),
        ],
        out_shape=[
            jax.ShapeDtypeStruct((rows, columns), F32),
            jax.ShapeDtypeStruct((copies, rows), F32),
        ],
        scratch_shapes=[pltpu.VMEM((rows, LANES), F32)],
        compiler_params=pltpu.CompilerParams(vmem_limit_bytes=VMEM_LIMIT),
        cost_estimate=pl.CostEstimate(
            flops=2 * rows * width * columns, bytes_accessed=6 * rows * columns, transcendentals=rows * columns
        ),
        name="first_sweep",
    )(*parts, protos)


def scale_rows(row_sums, row_scale):
    scale = 1.0 / jnp.sum(row_sums[...], axis=0, keepdims=True)
    row_scale[...] = jnp.broadcast_to(scale, (LANES, scale.shape[1])).T


def column_scale(plan, row_scale):
    scales = []
    for start in range(0, plan.shape[1], LANES):
        weighted = plan[:, start : start + LANES] * row_scale[...]
        scales.append(1.0 / jnp.sum(weighted, axis=0, keepdims=True))
    return scales


def sweep_kernel(row_sums, plan, sums, row_scale, partial):
    @pl.when(pl.program_id(0) == 0)
    def _():
        scale_rows(row_sums, row_scale)
        partial[...] = jnp.zeros_like(partial)

    scales = column_scale(plan, row_scale)
    total = partial[...]
    for j, scale in enumerate(scales):
        total = total + plan[:, j * LANES : (j + 1) * LANES] * scale
    partial[...] = total

    @pl.when(pl.program_id(0) == pl.num_programs(0) - 1)
    def _():
        sums[...] = jnp.broadcast_to(row_vector(partial[...]), sums.shape)


def sweep_call(row_sums, plan, block):
    copies = row_sums.shape[0]
    rows, columns = plan.shape
    return pl.pallas_call(
        sweep_kernel,
        grid=(columns // block,),
        in_specs=[
            pl.BlockSpec((copies, rows), lambda i: (0, 0)),
            pl.BlockSpec((rows, block), lambda i: (0, i)),
        ],
        out_specs=pl.BlockSpec((copies, rows), lambda i: (0, 0)),
        out_shape=jax.ShapeDtypeStruct((copies, rows), F32),
        scratch_shapes=[pltpu.VMEM((rows, LANES), F32)] * 2,
        compiler_params=pltpu.CompilerParams(vmem_limit_bytes=VMEM_LIMIT),
        cost_estimate=pl.CostEstimate(
            flops=4 * rows * columns, bytes_accessed=4 * rows * columns, transcendentals=0
        ),
        name="sweep",
    )(row_sums, plan)


def last_kernel(row_sums, plan, unit_protos, mixed, row_scale):
    own = mixed.shape[0]
    width = unit_protos.shape[0]

    @pl.when(pl.program_id(0) == 0)
    def _():
        scale_rows(row_sums, row_scale)
        mixed[...] = jnp.zeros_like(mixed)

    scales = column_scale(plan, row_scale)
    columns = [
        plan[:own, j * LANES : (j + 1) * LANES] * scale for j, scale in enumerate(scales)
    ]
    values = jnp.concatenate(columns, axis=1)
    mixed[:, width:] += lane_groups(values)
    mixed[:, :width] += dot_t(values.astype(BF16), unit_protos[...])


def last_call(row_sums, plan, unit_protos, own, block):
    copies = row_sums.shape[0]
    rows, columns = plan.shape
    width = unit_protos.shape[0]
    return pl.pallas_call(
        last_kernel,
        grid=(columns // block,),
        in_specs=[
            pl.BlockSpec((copies, rows), lambda i: (0, 0)),
            pl.BlockSpec((rows, block), lambda i: (0, i)),
            pl.BlockSpec((width, block), lambda i: (0, i)),
        ],
        out_specs=pl.BlockSpec((own, width + LANES), lambda i: (0, 0)),
        out_shape=jax.ShapeDtypeStruct((own, width + LANES), F32),
        scratch_shapes=[pltpu.VMEM((rows, LANES), F32)],
        compiler_params=pltpu.CompilerParams(vmem_limit_bytes=VMEM_LIMIT),
        cost_estimate=pl.CostEstimate(
            flops=2 * own * width * columns, bytes_accessed=6 * rows * columns, transcendentals=0
        ),
        name="last_sweep",
    )(row_sums, plan, unit_protos)


def mean_kernel(*refs):
    parts, out = refs[:-1], refs[-1]
    width = out.shape[1]
    total = parts[0][...]
    for part in parts[1:]:
        total = total + part[...]
    out[...] = total[:, :width] / jnp.sum(total[:, width:], axis=1, keepdims=True)


def mean_call(parts, width):
    rows = parts[0].shape[0]
    return pl.pallas_call(
        mean_kernel,
        out_shape=jax.ShapeDtypeStruct((rows, width), F32),
        compiler_params=pltpu.CompilerParams(vmem_limit_bytes=VMEM_LIMIT),
        name="mean_protos",
    )(*parts)


def finish_kernel(views, count, place, feats, picked, weights, back, *refs):
    parts, (gradient, loss, means) = refs[:count], refs[count:]
    width = means.shape[1]
    rows = parts[0].shape[0]
    for k, part in enumerate(parts):
        start = pl.multiple_of(jnp.bitwise_xor(place[0], k) * rows, rows)
        means[pl.ds(start, rows), :] = part[...]
    images = feats.shape[1]
    for crop in range(feats.shape[0]):
        raw = feats[crop].astype(F32)
        chosen = means[:images, :]
        for view in range(1, views):
            chosen = jnp.where(
                picked[:, crop : crop + 1] == view, means[view * images : (view + 1) * images, :], chosen
            )
        here = slice(crop * images, (crop + 1) * images)
        totals = jnp.sum(back[here, width:], axis=1, keepdims=True)
        factor = weights[:, crop : crop + 1] * (1.0 / student_softness)
        back_sum = factor * (back[here, :width] / totals - chosen)
        scales = lax.rsqrt(jnp.sum(raw * raw, axis=1, keepdims=True) + epsilon)
        along = jnp.sum(raw * back_sum, axis=1, keepdims=True)
        gradient[crop] = scales * back_sum - scales * scales * scales * raw * along
        unit = (raw * scales).astype(BF16).astype(F32)
        cross = jnp.sum(unit * chosen, axis=1, keepdims=True) * (1.0 / student_softness)
        column = jnp.log(totals) - cross
        loss[crop : crop + 1, :] = jnp.broadcast_to(column, (images, LANES)).T[:1, :]


def finish_call(views, place, feats, picked, weights, back, parts):
    crops, images, width = feats.shape
    vmem = pl.BlockSpec(memory_space=pltpu.VMEM)
    return pl.pallas_call(
        functools.partial(finish_kernel, views, len(parts)),
        in_specs=[pl.BlockSpec(memory_space=pltpu.SMEM)] + [vmem] * (4 + len(parts)),
        out_specs=[vmem, vmem],
        out_shape=[
            jax.ShapeDtypeStruct((crops, images, width), F32),
            jax.ShapeDtypeStruct((crops, images), F32),
        ],
        scratch_shapes=[pltpu.VMEM((views * images, width), F32)],
        compiler_params=pltpu.CompilerParams(vmem_limit_bytes=VMEM_LIMIT),
        name="finish",
    )(place, feats, picked, weights, back, *parts)


def swap(values, axis, distance):
    count = lax.axis_size(axis)
    return lax.ppermute(values, axis, [(i, i ^ distance) for i in range(count)])


def shards(teacher_feats, student_feats, teacher_protos, student_protos, pairing, row_weight):
    images, views, width = teacher_feats.shape
    crops = student_feats.shape[0]
    image_devices = lax.axis_size("image")
    crop_devices = lax.axis_size("crop")
    proto_devices = lax.axis_size("proto")
    place = lax.axis_index("crop")
    both = ("crop", "proto")
    block = 512

    own_rows = (
        unit_rows(jnp.swapaxes(teacher_feats, 0, 1).astype(F32)).astype(BF16).reshape(views * images, width)
    )
    teacher_parts = [own_rows] + [swap(own_rows, "image", k) for k in range(1, image_devices)]
    feats = student_feats.reshape(crops * images, width)
    student_parts = [feats] + [swap(feats, "crop", k) for k in range(1, crop_devices)]

    unit_protos, partial_back = student_call(student_parts, student_protos, block)
    rows = crops * images
    back = partial_back[:rows]
    for k in range(1, crop_devices):
        back = back + swap(partial_back[k * rows : (k + 1) * rows], "crop", k)
    back = lax.psum(back, "proto")

    plan, sums = first_call(teacher_parts, teacher_protos, crop_devices * proto_devices, block)
    for _ in range(SWEEPS - 2):
        sums = sweep_call(lax.all_to_all(sums, both, 0, 0), plan, block)
    mixed = last_call(lax.all_to_all(sums, both, 0, 0), plan, unit_protos, views * images, block)

    share = views * images // crop_devices
    half = lax.dynamic_slice_in_dim(mixed, place * share, share, 0)
    for k in range(1, crop_devices):
        half = half + swap(lax.dynamic_slice_in_dim(mixed, (place ^ k) * share, share, 0), "crop", k)
    means = mean_call([half] + [swap(half, "proto", k) for k in range(1, proto_devices)], width)
    means = [means] + [swap(means, "crop", k) for k in range(1, crop_devices)]
    return finish_call(
        views, place.reshape(1), student_feats, pairing.T, row_weight.T.astype(F32), back, means
    )


def solution(mesh):
    in_specs = (
        P("image", None, None),
        P("crop", "image", None),
        P(None, ("crop", "proto")),
        P(None, ("crop", "proto")),
        P("crop", "image"),
        P("crop", "image"),
    )
    out_specs = (P("crop", "image", None), P("crop", "image"))
    return jax.shard_map(shards, mesh=mesh, in_specs=in_specs, out_specs=out_specs, check_vma=False)
```

```python
import functools

import jax
import jax.numpy as jnp
from jax import lax
from jax.experimental import pallas as pl
from jax.experimental.pallas import tpu as pltpu
from jax.sharding import PartitionSpec as P

SWEEPS = 3
LANES = 128
ROW_TILE = 16
LEVELS = 32767.0
PARTS = 32768.0

epsilon = 1e-06
student_softness = 0.1
teacher_softness = 0.04

F32 = jnp.float32
BF16 = jnp.bfloat16
I16 = jnp.int16

IN_VMEM = pl.BlockSpec(memory_space=pltpu.VMEM)
IN_SMEM = pl.BlockSpec(memory_space=pltpu.SMEM)


def call(kernel, name, out_shape, scratch=(), scalars=0, vmem=16, after=(), flops=10**9, aliases=None):
    def run(*operands):
        count = len(operands)

        def body(*refs):
            kernel(*refs[:count], *refs[count + len(after) :])

        return pl.pallas_call(
            body,
            in_specs=[IN_SMEM] * scalars
            + [IN_VMEM] * (count - scalars)
            + [pl.BlockSpec(memory_space=pl.ANY)] * len(after),
            out_specs=jax.tree.map(lambda _: IN_VMEM, out_shape),
            out_shape=out_shape,
            scratch_shapes=list(scratch),
            compiler_params=pltpu.CompilerParams(vmem_limit_bytes=vmem * 1024 * 1024),
            cost_estimate=pl.CostEstimate(flops=flops, bytes_accessed=0, transcendentals=0),
            input_output_aliases=aliases or {},
            name=name,
        )(*operands, *after)

    return run


def shape(dims, dtype=F32):
    return jax.ShapeDtypeStruct(dims, dtype)


def unit_rows(raw_rows):
    return raw_rows * lax.rsqrt(jnp.sum(raw_rows * raw_rows, axis=-1, keepdims=True) + epsilon)


def unit_columns(entries):
    return entries * lax.rsqrt(jnp.sum(entries * entries, axis=0, keepdims=True) + epsilon)


def lane_groups(values):
    total = values[:, :LANES]
    for start in range(LANES, values.shape[1], LANES):
        total = total + values[:, start : start + LANES]
    return total


def dot_t(a, b):
    return lax.dot_general(a, b, (((1,), (1,)), ((), ())), preferred_element_type=F32)


def row_vector(partial):
    return jnp.sum(partial.T, axis=0, keepdims=True)


def tree_sum(terms):
    while len(terms) > 1:
        terms = [terms[i] + terms[i + 1] for i in range(0, len(terms), 2)]
    return terms[0]


def encode(values, extra):
    rows = values.shape[0]
    largest = jnp.maximum(jnp.max(jnp.abs(values), axis=1, keepdims=True), 1e-30)
    power = jnp.floor(jnp.log2(largest)) + 1.0
    whole = jnp.floor(values * (jnp.exp2(-power) * LEVELS) + 0.5)
    coded = jnp.clip(whole, -LEVELS, LEVELS).astype(jnp.int32).astype(I16)
    extra_power = jnp.floor(jnp.log2(jnp.maximum(extra, 1e-30))) + 1.0
    scaled = extra * jnp.exp2(-extra_power) * PARTS
    high = jnp.minimum(jnp.floor(scaled), LEVELS)
    low = jnp.minimum(jnp.floor((scaled - high) * PARTS), LEVELS)
    lane = lax.broadcasted_iota(jnp.int32, (rows, LANES), 1)
    tail = jnp.where(lane == 0, power, jnp.where(lane == 1, extra_power, jnp.where(lane == 2, high, low)))
    return coded, tail.astype(jnp.int32).astype(I16)


def store_code(out, values, extra):
    width = values.shape[1]
    out[:, :width], out[:, width:] = encode(values, extra)


def decode(ref):
    width = ref.shape[1] - LANES
    tail = ref[:, width:].astype(jnp.int32).astype(F32)
    values = ref[:, :width].astype(jnp.int32).astype(F32) * (jnp.exp2(tail[:, 0:1]) * (1.0 / LEVELS))
    extra = (tail[:, 2:3] + tail[:, 3:4] * (1.0 / PARTS)) * (1.0 / PARTS) * jnp.exp2(tail[:, 1:2])
    return values, extra


def decode_sum(refs):
    pairs = [decode(ref) for ref in refs]
    return tree_sum([p[0] for p in pairs]), tree_sum([p[1] for p in pairs])


def swap(values, axis, distance):
    count = lax.axis_size(axis)
    return lax.ppermute(values, axis, [(i, i ^ distance) for i in range(count)])


def student_kernel(count, block, place, feats, teacher_protos, *refs):
    protos, refs = refs[:count], refs[count:]
    unit_protos, unit_teacher = refs[:2]
    outs, (unit_feats, back) = refs[2:-2], refs[-2:]
    width, columns = unit_protos.shape
    unit_feats[...] = unit_rows(feats[...].astype(F32)).astype(BF16)
    for start in range(0, columns, block):
        here = slice(start, start + block)
        unit_teacher[:, here] = unit_columns(teacher_protos[:, here].astype(F32)).astype(BF16)
        for k, part in enumerate(protos):
            weights = unit_columns(part[:, here].astype(F32)).astype(BF16)
            if k == 0:
                unit_protos[:, here] = weights
            logits = jnp.dot(unit_feats[...], weights, preferred_element_type=F32)
            terms = jnp.exp(logits * (1.0 / student_softness))
            sums = lane_groups(terms)
            sides = dot_t(terms.astype(BF16), weights)
            if start == 0 and k == 0:
                back[:, width:] = sums
                back[:, :width] = sides
            else:
                back[:, width:] += sums
                back[:, :width] += sides
    share = outs[0].shape[0]
    for k, out in enumerate(outs):
        first = pl.multiple_of(jnp.bitwise_xor(place[0], k) * share, share)
        total = back[pl.ds(first, share), :]
        store_code(out, total[:, :width], lane_sums(total[:, width:]))


def student_call(place, feats, teacher_protos, protos, pieces, block):
    width, columns = teacher_protos.shape
    rows = feats.shape[0]
    out = call(
        functools.partial(student_kernel, len(protos), block),
        "student",
        [shape((width, columns), BF16)] * 2 + [shape((rows // pieces, width + LANES), I16)] * pieces,
        [pltpu.VMEM((rows, width), BF16), pltpu.VMEM((rows, width + LANES), F32)],
        scalars=1,
        vmem=48 if len(protos) > 2 else 16,
        flops=8 * rows * len(protos) * columns * width,
    )(place, feats, teacher_protos, *protos)
    return out[0], out[1], out[2:]


def first_kernel(count, block, *refs):
    parts, (weights, plan, sums, partial) = refs[:count], refs[count:]
    columns = weights.shape[1]
    for start in range(0, columns, block):
        here = slice(start, start + block)
        column_sums = None
        first = 0
        for part in parts:
            rows = part.shape[0]
            values = jnp.exp(
                jnp.dot(part[...], weights[:, here], preferred_element_type=F32) * (1.0 / teacher_softness)
            )
            plan[first : first + rows, here] = values
            total = jnp.sum(values, axis=0, keepdims=True)
            column_sums = total if column_sums is None else column_sums + total
            first += rows
        terms = lane_groups(plan[:, here] * (1.0 / column_sums))
        if start == 0:
            partial[...] = terms
        else:
            partial[...] += terms
    store_sums(sums, partial)


def store_sums(sums, partial):
    total = row_vector(partial[...])
    for k in range(sums.shape[0]):
        sums[k] = total


def first_call(parts, weights, copies, block, after=()):
    columns = weights.shape[1]
    rows = sum(part.shape[0] for part in parts)
    return call(
        functools.partial(first_kernel, len(parts), block),
        "first_sweep",
        [shape((rows, columns)), shape((copies, 1, rows))],
        [pltpu.VMEM((rows, LANES), F32)],
        after=after,
        flops=8 * rows * columns * weights.shape[0],
    )(*parts, weights)


def scale_rows(row_sums, row_scale):
    total = row_sums[0]
    for k in range(1, row_sums.shape[0]):
        total = total + row_sums[k]
    scale = 1.0 / total
    row_scale[...] = jnp.broadcast_to(scale, (LANES, scale.shape[1])).T


def column_scale(plan, row_scale, start):
    weighted = plan[:, start : start + LANES] * row_scale[...]
    return 1.0 / jnp.sum(weighted, axis=0, keepdims=True)


def sweep_kernel(row_sums, plan, *refs):
    shares, (sums, share, _, row_scale, partial) = refs[:-5], refs[-5:]
    back, totals = decode_sum(shares)
    store_code(share, back / totals, totals)
    scale_rows(row_sums, row_scale)
    for start in range(0, plan.shape[1], LANES):
        terms = plan[:, start : start + LANES] * column_scale(plan, row_scale, start)
        if start == 0:
            partial[...] = terms
        else:
            partial[...] += terms
    store_sums(sums, partial)


def sweep_call(row_sums, plan, shares):
    rows = plan.shape[0]
    return call(
        sweep_kernel,
        "sweep",
        [shape(row_sums.shape), shape(shares[0].shape, I16), shape(plan.shape)],
        [pltpu.VMEM((rows, LANES), F32)] * 2,
        aliases={1: 2},
    )(row_sums, plan, *shares)


def last_kernel(share, block, place, row_sums, plan, unit_protos, *refs):
    outs, (row_scale, scaled, mixed) = refs[:-3], refs[-3:]
    own = scaled.shape[0]
    width, columns = unit_protos.shape
    scale_rows(row_sums, row_scale)
    for start in range(0, columns, block):
        here = slice(start, start + block)
        total = None
        for group in range(start, start + block, LANES):
            terms = plan[:own, group : group + LANES] * column_scale(plan, row_scale, group)
            total = terms if total is None else total + terms
            scaled[:, group - start : group - start + LANES] = terms.astype(BF16)
        sides = dot_t(scaled[...], unit_protos[:, here])
        if start == 0:
            mixed[:, width:] = total
            mixed[:, :width] = sides
        else:
            mixed[:, width:] += total
            mixed[:, :width] += sides
    for k, out in enumerate(outs):
        first = pl.multiple_of(jnp.bitwise_xor(place[0], k) * share, share)
        out[...] = mixed[pl.ds(first, share), :]


def last_call(place, row_sums, plan, unit_protos, own, count, block, after=()):
    rows = plan.shape[0]
    width = unit_protos.shape[0]
    share = own // count
    return call(
        functools.partial(last_kernel, share, block),
        "last_sweep",
        [shape((share, width + LANES))] * count,
        [
            pltpu.VMEM((rows, LANES), F32),
            pltpu.VMEM((own, block), BF16),
            pltpu.VMEM((own, width + LANES), F32),
        ],
        scalars=1,
        after=after,
    )(place, row_sums, plan, unit_protos)


def lane_sums(values):
    return jnp.sum(values, axis=1, keepdims=True)


def code_kernel(*refs):
    parts, out = refs[:-1], refs[-1]
    width = out.shape[1] - LANES
    total = tree_sum([part[...] for part in parts])
    store_code(out, total[:, :width], lane_sums(total[:, width:]))


def code_call(parts, after=()):
    return call(code_kernel, "code_mixed", shape(parts[0].shape, I16), after=after)(*parts)


def mean_kernel(*refs):
    parts, out = refs[:-1], refs[-1]
    mixed, totals = decode_sum(parts)
    out[...] = mixed / totals


def mean_call(parts):
    rows, columns = parts[0].shape
    return call(mean_kernel, "mean_protos", shape((rows, columns - LANES)))(*parts)


def finish_kernel(views, mean_count, crop_place, proto_place, feats, picked, weights, *refs):
    parts, refs = refs[:mean_count], refs[mean_count:]
    shares, (gradient, loss, means, expected, totals) = refs[:-5], refs[-5:]
    rows = parts[0].shape[0]
    for k, part in enumerate(parts):
        first = pl.multiple_of(jnp.bitwise_xor(crop_place[0], k) * rows, rows)
        means[pl.ds(first, rows), :] = part[...]
    rows = shares[0].shape[0]
    for k, part in enumerate(shares):
        first = pl.multiple_of(jnp.bitwise_xor(proto_place[0], k) * rows, rows)
        values, extra = decode(part)
        expected[pl.ds(first, rows), :] = values
        totals[pl.ds(first, rows), :] = jnp.broadcast_to(extra, (rows, LANES))
    images = feats.shape[1]
    for crop in range(feats.shape[0]):
        raw = feats[crop].astype(F32)
        chosen = means[:images, :]
        for view in range(1, views):
            chosen = jnp.where(
                picked[:, crop : crop + 1] == view, means[view * images : (view + 1) * images, :], chosen
            )
        here = slice(crop * images, (crop + 1) * images)
        factor = weights[:, crop : crop + 1] * (1.0 / student_softness)
        back_sum = factor * (expected[here, :] - chosen)
        scales = lax.rsqrt(lane_sums(raw * raw) + epsilon)
        along = lane_sums(raw * back_sum)
        gradient[crop] = scales * back_sum - scales * scales * scales * raw * along
        unit = (raw * scales).astype(BF16).astype(F32)
        cross = lane_sums(unit * chosen) * (1.0 / student_softness)
        column = jnp.log(totals[here, 0:1]) - cross
        loss[crop : crop + 1, :] = jnp.broadcast_to(column, (images, LANES)).T[:1, :]


def finish_call(views, crop_place, proto_place, feats, picked, weights, means, shares):
    crops, images, width = feats.shape
    return call(
        functools.partial(finish_kernel, views, len(means)),
        "finish",
        [shape((crops, images, width)), shape((crops, images))],
        [
            pltpu.VMEM((views * images, width), F32),
            pltpu.VMEM((crops * images, width), F32),
            pltpu.VMEM((crops * images, LANES), F32),
        ],
        scalars=2,
    )(crop_place, proto_place, feats, picked, weights, *means, *shares)


def shards(teacher_feats, student_feats, teacher_protos, student_protos, pairing, row_weight):
    images, views, width = teacher_feats.shape
    crops = student_feats.shape[0]
    image_devices = lax.axis_size("image")
    crop_devices = lax.axis_size("crop")
    proto_devices = lax.axis_size("proto")
    crop_place = lax.axis_index("crop").reshape(1)
    proto_place = lax.axis_index("proto").reshape(1)
    both = ("crop", "proto")
    block = 512

    own_rows = (
        unit_rows(jnp.swapaxes(teacher_feats, 0, 1).astype(F32)).astype(BF16).reshape(views * images, width)
    )
    teacher_parts = [own_rows] + [swap(own_rows, "image", k) for k in range(1, image_devices)]
    feats = student_feats.reshape(crops * images, width)
    protos = [student_protos] + [swap(student_protos, "crop", k) for k in range(1, crop_devices)]

    pieces = proto_devices
    if crops * images % (pieces * ROW_TILE):
        pieces, proto_place = 1, jnp.zeros((1,), jnp.int32)
    unit_protos, unit_teacher, coded = student_call(
        proto_place, feats, teacher_protos, protos, pieces, block
    )
    plan, sums = first_call(teacher_parts, unit_teacher, crop_devices * proto_devices, block)
    shares = [coded[0]] + [swap(coded[k % pieces], "proto", k) for k in range(1, proto_devices)]
    for _ in range(SWEEPS - 2):
        sums, share, plan = sweep_call(lax.all_to_all(sums, both, 0, 0), plan, shares)
    shares = [share] + [swap(share, "proto", k) for k in range(1, pieces)]
    sums = lax.all_to_all(sums, both, 0, 0)
    mixed = last_call(
        crop_place, sums, plan, unit_protos, views * images, crop_devices, block, after=shares[1:]
    )

    mixed = code_call([mixed[0]] + [swap(mixed[k], "crop", k) for k in range(1, crop_devices)])
    means = mean_call([mixed] + [swap(mixed, "proto", k) for k in range(1, proto_devices)])
    means = [means] + [swap(means, "crop", k) for k in range(1, crop_devices)]
    return finish_call(
        views, crop_place, proto_place, student_feats, pairing.T, row_weight.T.astype(F32), means, shares
    )


def solution(mesh):
    in_specs = (
        P("image", None, None),
        P("crop", "image", None),
        P(None, ("crop", "proto")),
        P(None, ("crop", "proto")),
        P("crop", "image"),
        P("crop", "image"),
    )
    out_specs = (P("crop", "image", None), P("crop", "image"))
    return jax.shard_map(shards, mesh=mesh, in_specs=in_specs, out_specs=out_specs, check_vma=False)
```

```python
import functools

import jax
import jax.numpy as jnp
from jax import lax
from jax.experimental import pallas as pl
from jax.experimental.pallas import tpu as pltpu
from jax.sharding import PartitionSpec as P

SWEEPS = 3
LANES = 128
ROW_TILE = 16
LEVELS = 32767.0
PARTS = 32768.0

epsilon = 1e-06
student_softness = 0.1
teacher_softness = 0.04

F32 = jnp.float32
BF16 = jnp.bfloat16
I16 = jnp.int16

IN_VMEM = pl.BlockSpec(memory_space=pltpu.VMEM)
IN_HBM = pl.BlockSpec(memory_space=pltpu.HBM)
IN_SMEM = pl.BlockSpec(memory_space=pltpu.SMEM)


def call(kernel, name, out_shape, scratch=(), scalars=0, vmem=16, after=(), flops=10**9, aliases=None, far=()):
    def run(*operands):
        count = len(operands)

        def body(*refs):
            kernel(*refs[:count], *refs[count + len(after) :])

        return pl.pallas_call(
            body,
            in_specs=[IN_SMEM] * scalars
            + [IN_HBM if i in far else IN_VMEM for i in range(scalars, count)]
            + [pl.BlockSpec(memory_space=pl.ANY)] * len(after),
            out_specs=jax.tree.map(lambda _: IN_VMEM, out_shape),
            out_shape=out_shape,
            scratch_shapes=list(scratch),
            compiler_params=pltpu.CompilerParams(vmem_limit_bytes=vmem * 1024 * 1024),
            cost_estimate=pl.CostEstimate(flops=flops, bytes_accessed=0, transcendentals=0),
            input_output_aliases=aliases or {},
            name=name,
        )(*operands, *after)

    return run


def shape(dims, dtype=F32):
    return jax.ShapeDtypeStruct(dims, dtype)


def unit_rows(raw_rows):
    return raw_rows * lax.rsqrt(jnp.sum(raw_rows * raw_rows, axis=-1, keepdims=True) + epsilon)


def unit_columns(entries):
    return entries * lax.rsqrt(jnp.sum(entries * entries, axis=0, keepdims=True) + epsilon)


def lane_groups(values):
    total = values[:, :LANES]
    for start in range(LANES, values.shape[1], LANES):
        total = total + values[:, start : start + LANES]
    return total


def dot_t(a, b):
    return lax.dot_general(a, b, (((1,), (1,)), ((), ())), preferred_element_type=F32)


def row_vector(partial):
    return jnp.sum(partial.T, axis=0, keepdims=True)


def tree_sum(terms):
    while len(terms) > 1:
        terms = [terms[i] + terms[i + 1] for i in range(0, len(terms), 2)]
    return terms[0]


def encode(values, extra):
    rows = values.shape[0]
    largest = jnp.maximum(jnp.max(jnp.abs(values), axis=1, keepdims=True), 1e-30)
    power = jnp.floor(jnp.log2(largest)) + 1.0
    whole = jnp.floor(values * (jnp.exp2(-power) * LEVELS) + 0.5)
    coded = jnp.clip(whole, -LEVELS, LEVELS).astype(jnp.int32).astype(I16)
    extra_power = jnp.floor(jnp.log2(jnp.maximum(extra, 1e-30))) + 1.0
    scaled = extra * jnp.exp2(-extra_power) * PARTS
    high = jnp.minimum(jnp.floor(scaled), LEVELS)
    low = jnp.minimum(jnp.floor((scaled - high) * PARTS), LEVELS)
    lane = lax.broadcasted_iota(jnp.int32, (rows, LANES), 1)
    tail = jnp.where(lane == 0, power, jnp.where(lane == 1, extra_power, jnp.where(lane == 2, high, low)))
    return coded, tail.astype(jnp.int32).astype(I16)


def store_code(out, values, extra):
    width = values.shape[1]
    out[:, :width], out[:, width:] = encode(values, extra)


def decode(ref):
    width = ref.shape[1] - LANES
    tail = ref[:, width:].astype(jnp.int32).astype(F32)
    values = ref[:, :width].astype(jnp.int32).astype(F32) * (jnp.exp2(tail[:, 0:1]) * (1.0 / LEVELS))
    extra = (tail[:, 2:3] + tail[:, 3:4] * (1.0 / PARTS)) * (1.0 / PARTS) * jnp.exp2(tail[:, 1:2])
    return values, extra


def decode_sum(refs):
    pairs = [decode(ref) for ref in refs]
    return tree_sum([p[0] for p in pairs]), tree_sum([p[1] for p in pairs])


def swap(values, axis, distance):
    count = lax.axis_size(axis)
    return lax.ppermute(values, axis, [(i, i ^ distance) for i in range(count)])


def fetch(sources, buffers, sems, block):
    columns = buffers[0].shape[1]
    copies = []
    for j, start in enumerate(range(0, columns, block)):
        here = pl.ds(start, block)
        copies.append(
            [
                pltpu.make_async_copy(source.at[:, here], buffer.at[:, here], sems.at[i, j])
                for i, (source, buffer) in enumerate(zip(sources, buffers))
            ]
        )
    for group in copies:
        for copy in group:
            copy.start()
    return copies


def add_side(back, unit_feats, weights, fresh):
    width = weights.shape[0]
    logits = jnp.dot(unit_feats[...], weights, preferred_element_type=F32)
    terms = jnp.exp(logits * (1.0 / student_softness))
    sums = lane_groups(terms)
    sides = dot_t(terms.astype(BF16), weights)
    if fresh:
        back[:, width:] = sums
        back[:, :width] = sides
    else:
        back[:, width:] += sums
        back[:, :width] += sides


def own_kernel(block, crop_place, proto_place, feats, protos, teacher_protos, unit_protos, unit_teacher, unit_feats, back, *refs):
    raw, buffers, raw_sem, sems = refs[0], refs[1:3], refs[3], refs[4]
    raw_copy = pltpu.make_async_copy(feats, raw, raw_sem)
    raw_copy.start()
    copies = fetch([protos, teacher_protos], buffers, sems, block)
    raw_copy.wait()
    unit_feats[...] = unit_rows(raw[...].astype(F32)).astype(BF16)
    for j, group in enumerate(copies):
        here = slice(j * block, (j + 1) * block)
        group[0].wait()
        weights = unit_columns(buffers[0][:, here].astype(F32)).astype(BF16)
        unit_protos[:, here] = weights
        add_side(back, unit_feats, weights, j == 0)
        group[1].wait()
        unit_teacher[:, here] = unit_columns(buffers[1][:, here].astype(F32)).astype(BF16)


def own_call(crop_place, proto_place, feats, protos, teacher_protos, block):
    width, columns = protos.shape
    rows = feats.shape[0]
    return call(
        functools.partial(own_kernel, block),
        "student_own",
        [shape((width, columns), BF16)] * 2 + [shape((rows, width), BF16), shape((rows, width + LANES))],
        [pltpu.VMEM((rows, width), BF16)]
        + [pltpu.VMEM((width, columns), BF16)] * 2
        + [pltpu.SemaphoreType.DMA, pltpu.SemaphoreType.DMA((2, columns // block))],
        scalars=2,
        vmem=47,
        far=[2, 3, 4],
        flops=4 * rows * columns * width,
    )(crop_place, proto_place, feats, protos, teacher_protos)


def other_kernel(count, block, place, unit_feats, partial, *refs):
    sources, refs = refs[:count], refs[count:]
    outs, refs = refs[: -count - 2], refs[-count - 2 :]
    back, buffers, sems = refs[0], refs[1:-1], refs[-1]
    width = unit_feats.shape[1]
    copies = fetch(sources, buffers, sems, block)
    back[...] = partial[...]
    for j, group in enumerate(copies):
        here = slice(j * block, (j + 1) * block)
        for copy, buffer in zip(group, buffers):
            copy.wait()
            weights = unit_columns(buffer[:, here].astype(F32)).astype(BF16)
            add_side(back, unit_feats, weights, False)
    share = outs[0].shape[0]
    for k, out in enumerate(outs):
        first = pl.multiple_of(jnp.bitwise_xor(place[0], k) * share, share)
        total = back[pl.ds(first, share), :]
        store_code(out, total[:, :width], lane_sums(total[:, width:]))


def other_call(place, unit_feats, back, protos, pieces, block):
    width, columns = protos[0].shape
    rows = unit_feats.shape[0]
    count = len(protos)
    return call(
        functools.partial(other_kernel, count, block),
        "student_other",
        [shape((rows // pieces, width + LANES), I16)] * pieces,
        [pltpu.VMEM((rows, width + LANES), F32)]
        + [pltpu.VMEM((width, columns), BF16)] * count
        + [pltpu.SemaphoreType.DMA((count, columns // block))],
        scalars=1,
        vmem=48 if count > 1 else 16,
        far=range(3, 3 + count),
        flops=4 * rows * count * columns * width,
    )(place, unit_feats, back, *protos)


def first_kernel(count, block, *refs):
    parts, (weights, plan, sums, unit, partial) = refs[:count], refs[count:]
    columns = weights.shape[1]
    first = 0
    for part in parts:
        images, views, _ = part.shape
        for view in range(views):
            unit[first : first + images, :] = unit_rows(part[:, view, :].astype(F32)).astype(BF16)
            first += images
    for start in range(0, columns, block):
        here = slice(start, start + block)
        column_sums = None
        for first in range(0, unit.shape[0], LANES):
            values = jnp.exp(
                jnp.dot(unit[first : first + LANES, :], weights[:, here], preferred_element_type=F32)
                * (1.0 / teacher_softness)
            )
            plan[first : first + LANES, here] = values
            total = jnp.sum(values, axis=0, keepdims=True)
            column_sums = total if column_sums is None else column_sums + total
        terms = lane_groups(plan[:, here] * (1.0 / column_sums))
        if start == 0:
            partial[...] = terms
        else:
            partial[...] += terms
    store_sums(sums, partial)


def store_sums(sums, partial):
    total = row_vector(partial[...])
    for k in range(sums.shape[0]):
        sums[k] = total


def first_call(parts, weights, copies, block, after=()):
    columns = weights.shape[1]
    rows = sum(part.shape[0] * part.shape[1] for part in parts)
    return call(
        functools.partial(first_kernel, len(parts), block),
        "first_sweep",
        [shape((rows, columns)), shape((copies, 1, rows))],
        [pltpu.VMEM((rows, weights.shape[0]), BF16), pltpu.VMEM((rows, LANES), F32)],
        after=after,
        flops=8 * rows * columns * weights.shape[0],
    )(*parts, weights)


def scale_rows(row_sums, row_scale):
    total = row_sums[0]
    for k in range(1, row_sums.shape[0]):
        total = total + row_sums[k]
    scale = 1.0 / total
    row_scale[...] = jnp.broadcast_to(scale, (LANES, scale.shape[1])).T


def column_scale(plan, row_scale, start):
    weighted = plan[:, start : start + LANES] * row_scale[...]
    return 1.0 / jnp.sum(weighted, axis=0, keepdims=True)


def sweep_kernel(row_sums, plan, *refs):
    shares, (sums, share, _, row_scale, partial) = refs[:-5], refs[-5:]
    back, totals = decode_sum(shares)
    store_code(share, back / totals, totals)
    scale_rows(row_sums, row_scale)
    for start in range(0, plan.shape[1], LANES):
        terms = plan[:, start : start + LANES] * column_scale(plan, row_scale, start)
        if start == 0:
            partial[...] = terms
        else:
            partial[...] += terms
    store_sums(sums, partial)


def sweep_call(row_sums, plan, shares):
    rows = plan.shape[0]
    return call(
        sweep_kernel,
        "sweep",
        [shape(row_sums.shape), shape(shares[0].shape, I16), shape(plan.shape)],
        [pltpu.VMEM((rows, LANES), F32)] * 2,
        aliases={1: 2},
    )(row_sums, plan, *shares)


def last_kernel(share, block, place, row_sums, plan, unit_protos, *refs):
    outs, (row_scale, scaled, mixed) = refs[:-3], refs[-3:]
    own = scaled.shape[0]
    width, columns = unit_protos.shape
    scale_rows(row_sums, row_scale)
    for start in range(0, columns, block):
        here = slice(start, start + block)
        total = None
        for group in range(start, start + block, LANES):
            terms = plan[:own, group : group + LANES] * column_scale(plan, row_scale, group)
            total = terms if total is None else total + terms
            scaled[:, group - start : group - start + LANES] = terms.astype(BF16)
        sides = dot_t(scaled[...], unit_protos[:, here])
        if start == 0:
            mixed[:, width:] = total
            mixed[:, :width] = sides
        else:
            mixed[:, width:] += total
            mixed[:, :width] += sides
    for k, out in enumerate(outs):
        first = pl.multiple_of(jnp.bitwise_xor(place[0], k) * share, share)
        out[...] = mixed[pl.ds(first, share), :]


def last_call(place, row_sums, plan, unit_protos, own, count, block, after=()):
    rows = plan.shape[0]
    width = unit_protos.shape[0]
    share = own // count
    return call(
        functools.partial(last_kernel, share, block),
        "last_sweep",
        [shape((share, width + LANES))] * count,
        [
            pltpu.VMEM((rows, LANES), F32),
            pltpu.VMEM((own, block), BF16),
            pltpu.VMEM((own, width + LANES), F32),
        ],
        scalars=1,
        after=after,
    )(place, row_sums, plan, unit_protos)


def as_column(row):
    return jnp.broadcast_to(row, (LANES, row.shape[1])).T[:, :1]


def lane_sums(values):
    return jnp.sum(values, axis=1, keepdims=True)


def code_kernel(*refs):
    parts, out = refs[:-1], refs[-1]
    width = out.shape[1] - LANES
    total = tree_sum([part[...] for part in parts])
    store_code(out, total[:, :width], lane_sums(total[:, width:]))


def code_call(parts, after=()):
    return call(code_kernel, "code_mixed", shape(parts[0].shape, I16), after=after)(*parts)


def mean_kernel(*refs):
    parts, out = refs[:-1], refs[-1]
    mixed, totals = decode_sum(parts)
    out[...] = mixed / totals


def mean_call(parts):
    rows, columns = parts[0].shape
    return call(mean_kernel, "mean_protos", shape((rows, columns - LANES)))(*parts)


def finish_kernel(views, mean_count, crop_place, proto_place, feats, picked, weights, *refs):
    parts, refs = refs[:mean_count], refs[mean_count:]
    shares, (gradient, loss, means, expected, totals) = refs[:-5], refs[-5:]
    rows = parts[0].shape[0]
    for k, part in enumerate(parts):
        first = pl.multiple_of(jnp.bitwise_xor(crop_place[0], k) * rows, rows)
        means[pl.ds(first, rows), :] = part[...]
    rows = shares[0].shape[0]
    for k, part in enumerate(shares):
        first = pl.multiple_of(jnp.bitwise_xor(proto_place[0], k) * rows, rows)
        values, extra = decode(part)
        expected[pl.ds(first, rows), :] = values
        totals[pl.ds(first, rows), :] = jnp.broadcast_to(extra, (rows, LANES))
    images = feats.shape[1]
    for crop in range(feats.shape[0]):
        picked_column = as_column(picked[crop : crop + 1, :].astype(F32))
        weight_column = as_column(weights[crop : crop + 1, :].astype(F32))
        raw = feats[crop].astype(F32)
        chosen = means[:images, :]
        for view in range(1, views):
            chosen = jnp.where(
                picked_column == view, means[view * images : (view + 1) * images, :], chosen
            )
        here = slice(crop * images, (crop + 1) * images)
        factor = weight_column * (1.0 / student_softness)
        back_sum = factor * (expected[here, :] - chosen)
        scales = lax.rsqrt(lane_sums(raw * raw) + epsilon)
        along = lane_sums(raw * back_sum)
        gradient[crop] = scales * back_sum - scales * scales * scales * raw * along
        unit = (raw * scales).astype(BF16).astype(F32)
        cross = lane_sums(unit * chosen) * (1.0 / student_softness)
        column = jnp.log(totals[here, 0:1]) - cross
        loss[crop : crop + 1, :] = jnp.broadcast_to(column, (images, LANES)).T[:1, :]


def finish_call(views, crop_place, proto_place, feats, picked, weights, means, shares):
    crops, images, width = feats.shape
    return call(
        functools.partial(finish_kernel, views, len(means)),
        "finish",
        [shape((crops, images, width)), shape((crops, images))],
        [
            pltpu.VMEM((views * images, width), F32),
            pltpu.VMEM((crops * images, width), F32),
            pltpu.VMEM((crops * images, LANES), F32),
        ],
        scalars=2,
    )(crop_place, proto_place, feats, picked, weights, *means, *shares)


def shards(teacher_feats, student_feats, teacher_protos, student_protos, pairing, row_weight):
    images, views, width = teacher_feats.shape
    crops = student_feats.shape[0]
    image_devices = lax.axis_size("image")
    crop_devices = lax.axis_size("crop")
    proto_devices = lax.axis_size("proto")
    crop_place = lax.axis_index("crop").reshape(1)
    proto_place = lax.axis_index("proto").reshape(1)
    both = ("crop", "proto")
    block = 512

    teacher_parts = [teacher_feats] + [swap(teacher_feats, "image", k) for k in range(1, image_devices)]
    feats = student_feats.reshape(crops * images, width)
    protos = [student_protos] + [swap(student_protos, "crop", k) for k in range(1, crop_devices)]

    pieces = proto_devices
    if crops * images % (pieces * ROW_TILE):
        pieces, proto_place = 1, jnp.zeros((1,), jnp.int32)
    unit_protos, unit_teacher, unit_feats, back = own_call(
        crop_place, proto_place, feats, student_protos, teacher_protos, block
    )
    coded = other_call(proto_place, unit_feats, back, protos[1:], pieces, block)
    plan, sums = first_call(teacher_parts, unit_teacher, crop_devices * proto_devices, block)
    shares = [coded[0]] + [swap(coded[k % pieces], "proto", k) for k in range(1, proto_devices)]
    for _ in range(SWEEPS - 2):
        sums, share, plan = sweep_call(lax.all_to_all(sums, both, 0, 0), plan, shares)
    shares = [share] + [swap(share, "proto", k) for k in range(1, pieces)]
    sums = lax.all_to_all(sums, both, 0, 0)
    mixed = last_call(
        crop_place, sums, plan, unit_protos, views * images, crop_devices, block, after=shares[1:]
    )

    mixed = code_call([mixed[0]] + [swap(mixed[k], "crop", k) for k in range(1, crop_devices)])
    means = mean_call([mixed] + [swap(mixed, "proto", k) for k in range(1, proto_devices)])
    means = [means] + [swap(means, "crop", k) for k in range(1, crop_devices)]
    return finish_call(
        views, crop_place, proto_place, student_feats, pairing, row_weight, means, shares
    )


def solution(mesh):
    in_specs = (
        P("image", None, None),
        P("crop", "image", None),
        P(None, ("crop", "proto")),
        P(None, ("crop", "proto")),
        P("crop", "image"),
        P("crop", "image"),
    )
    out_specs = (P("crop", "image", None), P("crop", "image"))
    return jax.shard_map(shards, mesh=mesh, in_specs=in_specs, out_specs=out_specs, check_vma=False)
```

```python
import functools

import jax
import jax.numpy as jnp
from jax import lax
from jax.experimental import pallas as pl
from jax.experimental.pallas import tpu as pltpu
from jax.sharding import PartitionSpec as P

SWEEPS = 3
LANES = 128
ROW_TILE = 16
LEVELS = 32767.0
PARTS = 32768.0

epsilon = 1e-06
student_softness = 0.1
teacher_softness = 0.04

F32 = jnp.float32
BF16 = jnp.bfloat16
I16 = jnp.int16

IN_VMEM = pl.BlockSpec(memory_space=pltpu.VMEM)
IN_HBM = pl.BlockSpec(memory_space=pltpu.HBM)
IN_SMEM = pl.BlockSpec(memory_space=pltpu.SMEM)


def call(kernel, name, out_shape, scratch=(), scalars=0, vmem=16, after=(), flops=10**9, aliases=None, far=()):
    def run(*operands):
        count = len(operands)

        def body(*refs):
            kernel(*refs[:count], *refs[count + len(after) :])

        return pl.pallas_call(
            body,
            in_specs=[IN_SMEM] * scalars
            + [IN_HBM if i in far else IN_VMEM for i in range(scalars, count)]
            + [pl.BlockSpec(memory_space=pl.ANY)] * len(after),
            out_specs=jax.tree.map(lambda _: IN_VMEM, out_shape),
            out_shape=out_shape,
            scratch_shapes=list(scratch),
            compiler_params=pltpu.CompilerParams(vmem_limit_bytes=vmem * 1024 * 1024),
            cost_estimate=pl.CostEstimate(flops=flops, bytes_accessed=0, transcendentals=0),
            input_output_aliases=aliases or {},
            name=name,
        )(*operands, *after)

    return run


def shape(dims, dtype=F32):
    return jax.ShapeDtypeStruct(dims, dtype)


def unit_rows(raw_rows):
    return raw_rows * lax.rsqrt(jnp.sum(raw_rows * raw_rows, axis=-1, keepdims=True) + epsilon)


def unit_columns(entries):
    return entries * lax.rsqrt(jnp.sum(entries * entries, axis=0, keepdims=True) + epsilon)


def lane_groups(values):
    total = values[:, :LANES]
    for start in range(LANES, values.shape[1], LANES):
        total = total + values[:, start : start + LANES]
    return total


def dot_t(a, b):
    return lax.dot_general(a, b, (((1,), (1,)), ((), ())), preferred_element_type=F32)


def row_vector(partial):
    return jnp.sum(partial.T, axis=0, keepdims=True)


def tree_sum(terms):
    while len(terms) > 1:
        terms = [terms[i] + terms[i + 1] for i in range(0, len(terms), 2)]
    return terms[0]


def split_positive(values):
    power = jnp.floor(jnp.log2(jnp.maximum(values, 1e-30))) + 1.0
    scaled = values * jnp.exp2(-power) * PARTS
    high = jnp.minimum(jnp.floor(scaled), LEVELS)
    low = jnp.minimum(jnp.floor((scaled - high) * PARTS), LEVELS)
    return power, high, low


def join_positive(power, high, low):
    return (high + low * (1.0 / PARTS)) * (1.0 / PARTS) * jnp.exp2(power)


def to_i16(values):
    return values.astype(jnp.int32).astype(I16)


def to_f32(values):
    return values.astype(jnp.int32).astype(F32)


def store_code(out, values, extra):
    rows, width = values.shape
    largest = jnp.maximum(jnp.max(jnp.abs(values), axis=1, keepdims=True), 1e-30)
    power = jnp.floor(jnp.log2(largest)) + 1.0
    whole = jnp.floor(values * (jnp.exp2(-power) * LEVELS) + 0.5)
    out[:rows, :] = to_i16(jnp.clip(whole, -LEVELS, LEVELS))
    extra_power, high, low = split_positive(extra)
    lane = lax.broadcasted_iota(jnp.int32, (rows, LANES), 1)
    tail = jnp.where(lane == 0, power, jnp.where(lane == 1, extra_power, jnp.where(lane == 2, high, low)))
    if rows < LANES:
        tail = jnp.concatenate([tail, jnp.zeros((LANES - rows, LANES), F32)], axis=0)
    block = tail.T[:ROW_TILE, :]
    out[rows:, :] = to_i16(jnp.concatenate([block, jnp.zeros((ROW_TILE, width - LANES), F32)], axis=1))


def decode(ref):
    rows = ref.shape[0] - ROW_TILE
    block = to_f32(ref[rows:, :LANES])
    tail = jnp.concatenate([block, jnp.zeros((LANES - ROW_TILE, LANES), F32)], axis=0).T[:rows, :]
    values = to_f32(ref[:rows, :]) * (jnp.exp2(tail[:, 0:1]) * (1.0 / LEVELS))
    return values, join_positive(tail[:, 1:2], tail[:, 2:3], tail[:, 3:4])


def decode_sum(refs):
    pairs = [decode(ref) for ref in refs]
    return tree_sum([p[0] for p in pairs]), tree_sum([p[1] for p in pairs])


SUMS_AT = 4


def pack_kernel(count, *refs):
    parts, refs = refs[:count], refs[count:]
    shares, outs = refs[: len(refs) // 2], refs[len(refs) // 2 :]
    power, high, low = split_positive(tree_sum([part[0] for part in parts]))
    for share, out in zip(shares, outs):
        rows = share.shape[0] - ROW_TILE
        out[:rows, :] = share[:rows, :]
        at = lax.broadcasted_iota(jnp.int32, (ROW_TILE, share.shape[1]), 0)
        under = to_f32(share[rows:, :])
        for k, row in enumerate((power, high, low)):
            under = jnp.where(at == SUMS_AT + k, row, under)
        out[rows:, :] = to_i16(under)


def pack_call(parts, shares):
    return call(
        functools.partial(pack_kernel, len(parts)),
        "pack_sums",
        [shape(share.shape, I16) for share in shares],
    )(*parts, *shares)


def read_sums(refs):
    if refs[0].dtype == I16:
        terms = []
        for ref in refs:
            under = to_f32(ref[ref.shape[0] - ROW_TILE :, :])
            terms.append(join_positive(*(under[SUMS_AT + k : SUMS_AT + k + 1, :] for k in range(3))))
        return tree_sum(terms)
    total = refs[0][0]
    for k in range(1, refs[0].shape[0]):
        total = total + refs[0][k]
    return total


def swap(values, axis, distance):
    count = lax.axis_size(axis)
    return lax.ppermute(values, axis, [(i, i ^ distance) for i in range(count)])


def fetch(sources, buffers, sems, block):
    columns = buffers[0].shape[1]
    copies = []
    for j, start in enumerate(range(0, columns, block)):
        here = pl.ds(start, block)
        copies.append(
            [
                pltpu.make_async_copy(source.at[:, here], buffer.at[:, here], sems.at[i, j])
                for i, (source, buffer) in enumerate(zip(sources, buffers))
            ]
        )
    for group in copies:
        for copy in group:
            copy.start()
    return copies


def add_side(back, unit_feats, weights, fresh):
    width = weights.shape[0]
    logits = jnp.dot(unit_feats[...], weights, preferred_element_type=F32)
    terms = jnp.exp(logits * (1.0 / student_softness))
    sums = lane_groups(terms)
    sides = dot_t(terms.astype(BF16), weights)
    if fresh:
        back[:, width:] = sums
        back[:, :width] = sides
    else:
        back[:, width:] += sums
        back[:, :width] += sides


def own_kernel(block, crop_place, proto_place, feats, protos, teacher_protos, unit_protos, unit_teacher, unit_feats, back, *refs):
    raw, buffers, raw_sem, sems = refs[0], refs[1:3], refs[3], refs[4]
    raw_copy = pltpu.make_async_copy(feats, raw, raw_sem)
    raw_copy.start()
    copies = fetch([protos, teacher_protos], buffers, sems, block)
    raw_copy.wait()
    unit_feats[...] = unit_rows(raw[...].astype(F32)).astype(BF16)
    for j, group in enumerate(copies):
        here = slice(j * block, (j + 1) * block)
        group[0].wait()
        weights = unit_columns(buffers[0][:, here].astype(F32)).astype(BF16)
        unit_protos[:, here] = weights
        add_side(back, unit_feats, weights, j == 0)
        group[1].wait()
        unit_teacher[:, here] = unit_columns(buffers[1][:, here].astype(F32)).astype(BF16)


def own_call(crop_place, proto_place, feats, protos, teacher_protos, block):
    width, columns = protos.shape
    rows = feats.shape[0]
    return call(
        functools.partial(own_kernel, block),
        "student_own",
        [shape((width, columns), BF16)] * 2 + [shape((rows, width), BF16), shape((rows, width + LANES))],
        [pltpu.VMEM((rows, width), BF16)]
        + [pltpu.VMEM((width, columns), BF16)] * 2
        + [pltpu.SemaphoreType.DMA, pltpu.SemaphoreType.DMA((2, columns // block))],
        scalars=2,
        vmem=47,
        far=[2, 3, 4],
        flops=4 * rows * columns * width,
    )(crop_place, proto_place, feats, protos, teacher_protos)


def other_kernel(count, block, place, unit_feats, partial, *refs):
    sources, refs = refs[:count], refs[count:]
    outs, refs = refs[: -count - 2], refs[-count - 2 :]
    back, buffers, sems = refs[0], refs[1:-1], refs[-1]
    width = unit_feats.shape[1]
    copies = fetch(sources, buffers, sems, block)
    back[...] = partial[...]
    for j, group in enumerate(copies):
        here = slice(j * block, (j + 1) * block)
        for copy, buffer in zip(group, buffers):
            copy.wait()
            weights = unit_columns(buffer[:, here].astype(F32)).astype(BF16)
            add_side(back, unit_feats, weights, False)
    share = outs[0].shape[0] - ROW_TILE
    for k, out in enumerate(outs):
        first = pl.multiple_of(jnp.bitwise_xor(place[0], k) * share, share)
        total = back[pl.ds(first, share), :]
        store_code(out, total[:, :width], lane_sums(total[:, width:]))


def other_call(place, unit_feats, back, protos, pieces, block):
    width, columns = protos[0].shape
    rows = unit_feats.shape[0]
    count = len(protos)
    return call(
        functools.partial(other_kernel, count, block),
        "student_other",
        [shape((rows // pieces + ROW_TILE, width), I16)] * pieces,
        [pltpu.VMEM((rows, width + LANES), F32)]
        + [pltpu.VMEM((width, columns), BF16)] * count
        + [pltpu.SemaphoreType.DMA((count, columns // block))],
        scalars=1,
        vmem=48 if count > 1 else 16,
        far=range(3, 3 + count),
        flops=4 * rows * count * columns * width,
    )(place, unit_feats, back, *protos)


def first_kernel(count, block, *refs):
    parts, (weights, plan, sums, unit, partial) = refs[:count], refs[count:]
    columns = weights.shape[1]
    first = 0
    for part in parts:
        images, views, _ = part.shape
        for view in range(views):
            unit[first : first + images, :] = unit_rows(part[:, view, :].astype(F32)).astype(BF16)
            first += images
    for start in range(0, columns, block):
        here = slice(start, start + block)
        column_sums = None
        for first in range(0, unit.shape[0], LANES):
            values = jnp.exp(
                jnp.dot(unit[first : first + LANES, :], weights[:, here], preferred_element_type=F32)
                * (1.0 / teacher_softness)
            )
            plan[first : first + LANES, here] = values
            total = jnp.sum(values, axis=0, keepdims=True)
            column_sums = total if column_sums is None else column_sums + total
        terms = lane_groups(plan[:, here] * (1.0 / column_sums))
        if start == 0:
            partial[...] = terms
        else:
            partial[...] += terms
    store_sums(sums, partial)


def store_sums(sums, partial):
    total = row_vector(partial[...])
    for k in range(sums.shape[0]):
        sums[k] = total


def first_call(parts, weights, copies, block, after=()):
    columns = weights.shape[1]
    rows = sum(part.shape[0] * part.shape[1] for part in parts)
    return call(
        functools.partial(first_kernel, len(parts), block),
        "first_sweep",
        [shape((rows, columns)), shape((copies, 1, rows))],
        [pltpu.VMEM((rows, weights.shape[0]), BF16), pltpu.VMEM((rows, LANES), F32)],
        after=after,
        flops=8 * rows * columns * weights.shape[0],
    )(*parts, weights)


def scale_rows(sum_refs, row_scale):
    scale = 1.0 / read_sums(sum_refs)
    row_scale[...] = jnp.broadcast_to(scale, (LANES, scale.shape[1])).T


def column_scale(plan, row_scale, start):
    weighted = plan[:, start : start + LANES] * row_scale[...]
    return 1.0 / jnp.sum(weighted, axis=0, keepdims=True)


def sweep_kernel(count, plan, *refs):
    shares, refs = refs[:count], refs[count:]
    sum_refs, (sums, share, _, row_scale, partial) = refs[:-5] or shares, refs[-5:]
    scale_rows(sum_refs, row_scale)
    for start in range(0, plan.shape[1], LANES):
        terms = plan[:, start : start + LANES] * column_scale(plan, row_scale, start)
        if start == 0:
            partial[...] = terms
        else:
            partial[...] += terms
    store_sums(sums, partial)
    back, totals = decode_sum(shares)
    store_code(share, back / totals, totals)


def sweep_call(plan, copies, shares, row_sums):
    rows = plan.shape[0]
    return call(
        functools.partial(sweep_kernel, len(shares)),
        "sweep",
        [shape((copies, 1, rows)), shape(shares[0].shape, I16), shape(plan.shape)],
        [pltpu.VMEM((rows, LANES), F32)] * 2,
        aliases={0: 2},
    )(plan, *shares, *row_sums)


def last_kernel(share, count, block, place, plan, unit_protos, *refs):
    sum_refs, refs = refs[:count], refs[count:]
    outs, (row_scale, scaled, mixed) = refs[:-3], refs[-3:]
    own = scaled.shape[0]
    width, columns = unit_protos.shape
    scale_rows(sum_refs, row_scale)
    for start in range(0, columns, block):
        here = slice(start, start + block)
        total = None
        for group in range(start, start + block, LANES):
            terms = plan[:own, group : group + LANES] * column_scale(plan, row_scale, group)
            total = terms if total is None else total + terms
            scaled[:, group - start : group - start + LANES] = terms.astype(BF16)
        sides = dot_t(scaled[...], unit_protos[:, here])
        if start == 0:
            mixed[:, width:] = total
            mixed[:, :width] = sides
        else:
            mixed[:, width:] += total
            mixed[:, :width] += sides
    for k, out in enumerate(outs):
        first = pl.multiple_of(jnp.bitwise_xor(place[0], k) * share, share)
        out[...] = mixed[pl.ds(first, share), :]


def last_call(place, plan, unit_protos, sums, own, count, block, after=()):
    rows = plan.shape[0]
    width = unit_protos.shape[0]
    share = own // count
    return call(
        functools.partial(last_kernel, share, len(sums), block),
        "last_sweep",
        [shape((share, width + LANES))] * count,
        [
            pltpu.VMEM((rows, LANES), F32),
            pltpu.VMEM((own, block), BF16),
            pltpu.VMEM((own, width + LANES), F32),
        ],
        scalars=1,
        after=after,
    )(place, plan, unit_protos, *sums)


def as_column(row):
    return jnp.broadcast_to(row, (LANES, row.shape[1])).T[:, :1]


def lane_sums(values):
    return jnp.sum(values, axis=1, keepdims=True)


def code_kernel(*refs):
    parts, out = refs[:-1], refs[-1]
    width = out.shape[1]
    total = tree_sum([part[...] for part in parts])
    store_code(out, total[:, :width], lane_sums(total[:, width:]))


def code_call(parts, after=()):
    rows, columns = parts[0].shape
    out = shape((rows + ROW_TILE, columns - LANES), I16)
    return call(code_kernel, "code_mixed", out, after=after)(*parts)


def mean_kernel(*refs):
    parts, out = refs[:-1], refs[-1]
    mixed, totals = decode_sum(parts)
    out[...] = mixed / totals


def mean_call(parts, after=()):
    rows, width = parts[0].shape
    return call(mean_kernel, "mean_protos", shape((rows - ROW_TILE, width)), after=after)(*parts)


FIELDS = 4


def prepare_kernel(place, feats, picked, weights, *refs):
    shares, (base, fields, expected, totals) = refs[:-4], refs[-4:]
    rows = shares[0].shape[0] - ROW_TILE
    for k, part in enumerate(shares):
        first = pl.multiple_of(jnp.bitwise_xor(place[0], k) * rows, rows)
        values, extra = decode(part)
        expected[pl.ds(first, rows), :] = values
        totals[pl.ds(first, rows), :] = jnp.broadcast_to(extra, (rows, LANES))
    images = feats.shape[1]
    lane = lax.broadcasted_iota(jnp.int32, (images, LANES), 1)
    for crop in range(feats.shape[0]):
        here = slice(crop * images, (crop + 1) * images)
        raw = feats[crop].astype(F32)
        scales = lax.rsqrt(lane_sums(raw * raw) + epsilon)
        factor = as_column(weights[crop : crop + 1, :].astype(F32)) * (scales * (1.0 / student_softness))
        cubic = factor * scales * scales
        mean = expected[here, :]
        base[here, :] = factor * mean - (cubic * lane_sums(raw * mean)) * raw
        logs = jnp.log(totals[here, :])
        view = as_column(picked[crop : crop + 1, :].astype(F32))
        fields[here, :] = jnp.where(
            lane == 0, factor, jnp.where(lane == 1, cubic, jnp.where(lane == 2, scales, logs))
        )
        fields[here, :] = jnp.where(lane == FIELDS, view, fields[here, :])


def prepare_call(place, feats, picked, weights, shares, after=()):
    crops, images, width = feats.shape
    rows = crops * images
    return call(
        prepare_kernel,
        "prepare",
        [shape((rows, width)), shape((rows, LANES))],
        [pltpu.VMEM((rows, width), F32), pltpu.VMEM((rows, LANES), F32)],
        scalars=1,
        after=after,
    )(place, feats, picked, weights, *shares)


def finish_kernel(views, place, feats, base, fields, *refs):
    parts, (gradient, loss, means) = refs[:-3], refs[-3:]
    rows = parts[0].shape[0]
    for k, part in enumerate(parts):
        first = pl.multiple_of(jnp.bitwise_xor(place[0], k) * rows, rows)
        means[pl.ds(first, rows), :] = part[...]
    images = feats.shape[1]
    for crop in range(feats.shape[0]):
        here = slice(crop * images, (crop + 1) * images)
        raw = feats[crop].astype(F32)
        factor, cubic, scales = (fields[here, k : k + 1] for k in range(3))
        view_column = fields[here, FIELDS : FIELDS + 1]
        chosen = means[:images, :]
        for view in range(1, views):
            chosen = jnp.where(view_column == view, means[view * images : (view + 1) * images, :], chosen)
        along = cubic * lane_sums(raw * chosen)
        gradient[crop] = base[here, :] - factor * chosen + along * raw
        unit = (raw * scales).astype(BF16).astype(F32)
        column = fields[here, FIELDS - 1 : FIELDS] - lane_sums(unit * chosen) * (1.0 / student_softness)
        loss[crop : crop + 1, :] = jnp.broadcast_to(column, (images, LANES)).T[:1, :]


def finish_call(views, place, feats, base, fields, means):
    crops, images, width = feats.shape
    return call(
        functools.partial(finish_kernel, views),
        "finish",
        [shape((crops, images, width)), shape((crops, images))],
        [pltpu.VMEM((views * images, width), F32)],
        scalars=1,
    )(place, feats, base, fields, *means)


def shards(teacher_feats, student_feats, teacher_protos, student_protos, pairing, row_weight):
    images, views, width = teacher_feats.shape
    crops = student_feats.shape[0]
    image_devices = lax.axis_size("image")
    crop_devices = lax.axis_size("crop")
    proto_devices = lax.axis_size("proto")
    crop_place = lax.axis_index("crop").reshape(1)
    proto_place = lax.axis_index("proto").reshape(1)
    block = 512

    teacher_parts = [teacher_feats] + [swap(teacher_feats, "image", k) for k in range(1, image_devices)]
    feats = student_feats.reshape(crops * images, width)
    protos = [student_protos] + [swap(student_protos, "crop", k) for k in range(1, crop_devices)]

    teacher_rows = image_devices * images * views
    joint = crops * images % (proto_devices * ROW_TILE) == 0 and teacher_rows == width
    pieces, copies = (proto_devices, 1) if joint else (1, crop_devices * proto_devices)
    if not joint:
        proto_place = jnp.zeros((1,), jnp.int32)

    def from_all(shares):
        return [shares[0]] + [swap(shares[k % len(shares)], "proto", k) for k in range(1, proto_devices)]

    def exchange(sums, shares):
        if joint:
            parts = [sums] + [swap(sums, "crop", k) for k in range(1, crop_devices)]
            return from_all(pack_call(parts, shares)), []
        return from_all(shares), [lax.all_to_all(sums, ("crop", "proto"), 0, 0)]

    unit_protos, unit_teacher, unit_feats, back = own_call(
        crop_place, proto_place, feats, student_protos, teacher_protos, block
    )
    shares = other_call(proto_place, unit_feats, back, protos[1:], pieces, block)
    plan, sums = first_call(teacher_parts, unit_teacher, copies, block)
    for _ in range(SWEEPS - 2):
        shares, row_sums = exchange(sums, shares)
        sums, share, plan = sweep_call(plan, copies, shares, row_sums)
        shares = [share]
    if joint:
        shares, row_sums = exchange(sums, shares)
    else:
        row_sums = [lax.all_to_all(sums, ("crop", "proto"), 0, 0)]
    mixed = last_call(
        crop_place, plan, unit_protos, row_sums or shares, views * images, crop_devices, block
    )

    coded = code_call([mixed[0]] + [swap(mixed[k], "crop", k) for k in range(1, crop_devices)])
    base, fields = prepare_call(proto_place, student_feats, pairing, row_weight, shares, after=[coded])
    means = mean_call(from_all([coded]), after=[base])
    means = [means] + [swap(means, "crop", k) for k in range(1, crop_devices)]
    return finish_call(views, crop_place, student_feats, base, fields, means)


def solution(mesh):
    in_specs = (
        P("image", None, None),
        P("crop", "image", None),
        P(None, ("crop", "proto")),
        P(None, ("crop", "proto")),
        P("crop", "image"),
        P("crop", "image"),
    )
    out_specs = (P("crop", "image", None), P("crop", "image"))
    return jax.shard_map(shards, mesh=mesh, in_specs=in_specs, out_specs=out_specs, check_vma=False)
```

```python
import functools

import jax
import jax.numpy as jnp
from jax import lax
from jax.experimental import pallas as pl
from jax.experimental.pallas import tpu as pltpu
from jax.sharding import PartitionSpec as P

LANES = 128
ROW_TILE = 16
LEVELS = 32767.0
PARTS = 32768.0

epsilon = 1e-06
student_softness = 0.1
teacher_softness = 0.04

F32 = jnp.float32
BF16 = jnp.bfloat16
I16 = jnp.int16

IN_VMEM = pl.BlockSpec(memory_space=pltpu.VMEM)
IN_HBM = pl.BlockSpec(memory_space=pltpu.HBM)
IN_SMEM = pl.BlockSpec(memory_space=pltpu.SMEM)


def call(kernel, name, out_shape, scratch=(), scalars=0, vmem=16, after=(), flops=10**9, aliases=None, far=()):
    def run(*operands):
        count = len(operands)

        def body(*refs):
            kernel(*refs[:count], *refs[count + len(after) :])

        return pl.pallas_call(
            body,
            in_specs=[IN_SMEM] * scalars
            + [IN_HBM if i in far else IN_VMEM for i in range(scalars, count)]
            + [pl.BlockSpec(memory_space=pl.ANY)] * len(after),
            out_specs=jax.tree.map(lambda _: IN_VMEM, out_shape),
            out_shape=out_shape,
            scratch_shapes=list(scratch),
            compiler_params=pltpu.CompilerParams(vmem_limit_bytes=vmem * 1024 * 1024),
            cost_estimate=pl.CostEstimate(flops=flops, bytes_accessed=0, transcendentals=0),
            input_output_aliases=aliases or {},
            name=name,
        )(*operands, *after)

    return run


def shape(dims, dtype=F32):
    return jax.ShapeDtypeStruct(dims, dtype)


def unit_rows(raw_rows):
    return raw_rows * lax.rsqrt(jnp.sum(raw_rows * raw_rows, axis=-1, keepdims=True) + epsilon)


def unit_columns(entries):
    return entries * lax.rsqrt(jnp.sum(entries * entries, axis=0, keepdims=True) + epsilon)


def lane_groups(values):
    total = values[:, :LANES]
    for start in range(LANES, values.shape[1], LANES):
        total = total + values[:, start : start + LANES]
    return total


def dot_t(a, b):
    return lax.dot_general(a, b, (((1,), (1,)), ((), ())), preferred_element_type=F32)


def row_vector(partial):
    return jnp.sum(partial.T, axis=0, keepdims=True)


def tree_sum(terms):
    while len(terms) > 1:
        terms = [terms[i] + terms[i + 1] for i in range(0, len(terms), 2)]
    return terms[0]


def split_positive(values):
    power = jnp.floor(jnp.log2(jnp.maximum(values, 1e-30))) + 1.0
    scaled = values * jnp.exp2(-power) * PARTS
    high = jnp.minimum(jnp.floor(scaled), LEVELS)
    low = jnp.minimum(jnp.floor((scaled - high) * PARTS), LEVELS)
    return power, high, low


def join_positive(power, high, low):
    return (high + low * (1.0 / PARTS)) * (1.0 / PARTS) * jnp.exp2(power)


def to_i16(values):
    return values.astype(jnp.int32).astype(I16)


def to_f32(values):
    return values.astype(jnp.int32).astype(F32)


def store_code(out, values, extra):
    rows, width = values.shape
    largest = jnp.maximum(jnp.max(jnp.abs(values), axis=1, keepdims=True), 1e-30)
    power = jnp.floor(jnp.log2(largest)) + 1.0
    whole = jnp.floor(values * (jnp.exp2(-power) * LEVELS) + 0.5)
    out[:rows, :] = to_i16(jnp.clip(whole, -LEVELS, LEVELS))
    extra_power, high, low = split_positive(extra)
    lane = lax.broadcasted_iota(jnp.int32, (rows, LANES), 1)
    tail = jnp.where(lane == 0, power, jnp.where(lane == 1, extra_power, jnp.where(lane == 2, high, low)))
    if rows < LANES:
        tail = jnp.concatenate([tail, jnp.zeros((LANES - rows, LANES), F32)], axis=0)
    block = tail.T[:ROW_TILE, :]
    out[rows:, :] = to_i16(jnp.concatenate([block, jnp.zeros((ROW_TILE, width - LANES), F32)], axis=1))


def decode(ref):
    rows = ref.shape[0] - ROW_TILE
    block = to_f32(ref[rows:, :LANES])
    tail = jnp.concatenate([block, jnp.zeros((LANES - ROW_TILE, LANES), F32)], axis=0).T[:rows, :]
    values = to_f32(ref[:rows, :]) * (jnp.exp2(tail[:, 0:1]) * (1.0 / LEVELS))
    return values, join_positive(tail[:, 1:2], tail[:, 2:3], tail[:, 3:4])


def decode_sum(refs):
    pairs = [decode(ref) for ref in refs]
    return tree_sum([p[0] for p in pairs]), tree_sum([p[1] for p in pairs])


def join_kernel(count, at, *refs):
    refs[at][...] = tree_sum([part[...] for part in refs[:count]])


def join_call(parts, shares):
    count = len(parts)
    out = call(
        functools.partial(join_kernel, count, count + len(shares)),
        "join_sums",
        [shape(parts[0].shape)] + [shape(share.shape, I16) for share in shares],
        aliases={count + i: 1 + i for i in range(len(shares))},
    )(*parts, *shares)
    return out[0], out[1:]


def join_kernel(count, at, *refs):
    refs[at][...] = tree_sum([part[...] for part in refs[:count]])


def join_call(parts, shares):
    count = len(parts)
    out = call(
        functools.partial(join_kernel, count, count + len(shares)),
        "join_sums",
        [shape(parts[0].shape)] + [shape(share.shape, I16) for share in shares],
        aliases={count + i: 1 + i for i in range(len(shares))},
    )(*parts, *shares)
    return out[0], out[1:]


def read_sums(refs):
    terms = [ref[k] for ref in refs for k in range(ref.shape[0])]
    return tree_sum(terms)


def swap(values, axis, distance):
    count = lax.axis_size(axis)
    return lax.ppermute(values, axis, [(i, i ^ distance) for i in range(count)])


def fetch(sources, buffers, sems, block):
    columns = buffers[0].shape[1]
    copies = []
    for j, start in enumerate(range(0, columns, block)):
        here = pl.ds(start, block)
        copies.append(
            [
                pltpu.make_async_copy(source.at[:, here], buffer.at[:, here], sems.at[i, j])
                for i, (source, buffer) in enumerate(zip(sources, buffers))
            ]
        )
    for group in copies:
        for copy in group:
            copy.start()
    return copies


def add_side(back, unit_feats, weights, fresh):
    width = weights.shape[0]
    logits = jnp.dot(unit_feats[...], weights, preferred_element_type=F32)
    terms = jnp.exp(logits * (1.0 / student_softness))
    sums = lane_groups(terms)
    sides = dot_t(terms.astype(BF16), weights)
    if fresh:
        back[:, width:] = sums
        back[:, :width] = sides
    else:
        back[:, width:] += sums
        back[:, :width] += sides


def own_kernel(block, crop_place, proto_place, feats, protos, teacher_protos, unit_protos, unit_teacher, unit_feats, back, *refs):
    raw, buffers, raw_sem, sems = refs[0], refs[1:3], refs[3], refs[4]
    raw_copy = pltpu.make_async_copy(feats, raw, raw_sem)
    raw_copy.start()
    copies = fetch([protos, teacher_protos], buffers, sems, block)
    raw_copy.wait()
    unit_feats[...] = unit_rows(raw[...].astype(F32)).astype(BF16)
    for j, group in enumerate(copies):
        here = slice(j * block, (j + 1) * block)
        group[0].wait()
        weights = unit_columns(buffers[0][:, here].astype(F32)).astype(BF16)
        unit_protos[:, here] = weights
        add_side(back, unit_feats, weights, j == 0)
        group[1].wait()
        unit_teacher[:, here] = unit_columns(buffers[1][:, here].astype(F32)).astype(BF16)


def own_call(crop_place, proto_place, feats, protos, teacher_protos, block):
    width, columns = protos.shape
    rows = feats.shape[0]
    return call(
        functools.partial(own_kernel, block),
        "student_own",
        [shape((width, columns), BF16)] * 2 + [shape((rows, width), BF16), shape((rows, width + LANES))],
        [pltpu.VMEM((rows, width), BF16)]
        + [pltpu.VMEM((width, columns), BF16)] * 2
        + [pltpu.SemaphoreType.DMA, pltpu.SemaphoreType.DMA((2, columns // block))],
        scalars=2,
        vmem=47,
        far=[2, 3, 4],
        flops=4 * rows * columns * width,
    )(crop_place, proto_place, feats, protos, teacher_protos)


def other_kernel(count, block, place, unit_feats, partial, *refs):
    sources, refs = refs[:count], refs[count:]
    outs, refs = refs[: -count - 2], refs[-count - 2 :]
    back, buffers, sems = refs[0], refs[1:-1], refs[-1]
    width = unit_feats.shape[1]
    copies = fetch(sources, buffers, sems, block)
    back[...] = partial[...]
    for j, group in enumerate(copies):
        here = slice(j * block, (j + 1) * block)
        for copy, buffer in zip(group, buffers):
            copy.wait()
            weights = unit_columns(buffer[:, here].astype(F32)).astype(BF16)
            add_side(back, unit_feats, weights, False)
    share = outs[0].shape[0] - ROW_TILE
    for k, out in enumerate(outs):
        first = pl.multiple_of(jnp.bitwise_xor(place[0], k) * share, share)
        total = back[pl.ds(first, share), :]
        store_code(out, total[:, :width], lane_sums(total[:, width:]))


def other_call(place, unit_feats, back, protos, pieces, block):
    width, columns = protos[0].shape
    rows = unit_feats.shape[0]
    count = len(protos)
    return call(
        functools.partial(other_kernel, count, block),
        "student_other",
        [shape((rows // pieces + ROW_TILE, width), I16)] * pieces,
        [pltpu.VMEM((rows, width + LANES), F32)]
        + [pltpu.VMEM((width, columns), BF16)] * count
        + [pltpu.SemaphoreType.DMA((count, columns // block))],
        scalars=1,
        vmem=48 if count > 1 else 16,
        far=range(3, 3 + count),
        flops=4 * rows * count * columns * width,
    )(place, unit_feats, back, *protos)


def first_kernel(count, block, *refs):
    parts, (weights, plan, sums, unit, partial) = refs[:count], refs[count:]
    columns = weights.shape[1]
    first = 0
    for part in parts:
        images, views, _ = part.shape
        for view in range(views):
            unit[first : first + images, :] = unit_rows(part[:, view, :].astype(F32)).astype(BF16)
            first += images
    for start in range(0, columns, block):
        here = slice(start, start + block)
        column_sums = None
        for first in range(0, unit.shape[0], LANES):
            values = jnp.exp(
                jnp.dot(unit[first : first + LANES, :], weights[:, here], preferred_element_type=F32)
                * (1.0 / teacher_softness)
            )
            plan[first : first + LANES, here] = values
            total = jnp.sum(values, axis=0, keepdims=True)
            column_sums = total if column_sums is None else column_sums + total
        terms = lane_groups(plan[:, here] * (1.0 / column_sums))
        if start == 0:
            partial[...] = terms
        else:
            partial[...] += terms
    store_sums(sums, partial)


def store_sums(sums, partial):
    total = row_vector(partial[...])
    for k in range(sums.shape[0]):
        sums[k] = total


def first_call(parts, weights, copies, block, after=()):
    columns = weights.shape[1]
    rows = sum(part.shape[0] * part.shape[1] for part in parts)
    return call(
        functools.partial(first_kernel, len(parts), block),
        "first_sweep",
        [shape((rows, columns)), shape((copies, 1, rows))],
        [pltpu.VMEM((rows, weights.shape[0]), BF16), pltpu.VMEM((rows, LANES), F32)],
        after=after,
        flops=8 * rows * columns * weights.shape[0],
    )(*parts, weights)


def scale_rows(sum_refs, row_scale):
    scale = 1.0 / read_sums(sum_refs)
    row_scale[...] = jnp.broadcast_to(scale, (LANES, scale.shape[1])).T


def column_scale(plan, row_scale, start):
    weighted = plan[:, start : start + LANES] * row_scale[...]
    return 1.0 / jnp.sum(weighted, axis=0, keepdims=True)


def sweep_kernel(plan, *refs):
    sum_refs, (sums, _, row_scale, partial) = refs[:-4], refs[-4:]
    scale_rows(sum_refs, row_scale)
    for start in range(0, plan.shape[1], LANES):
        terms = plan[:, start : start + LANES] * column_scale(plan, row_scale, start)
        if start == 0:
            partial[...] = terms
        else:
            partial[...] += terms
    store_sums(sums, partial)


def sweep_call(plan, copies, row_sums):
    rows = plan.shape[0]
    return call(
        sweep_kernel,
        "sweep",
        [shape((copies, 1, rows)), shape(plan.shape)],
        [pltpu.VMEM((rows, LANES), F32)] * 2,
        aliases={0: 1},
        flops=10**10,
    )(plan, *row_sums)


def total_kernel(*refs):
    shares, share = refs[:-1], refs[-1]
    back, totals = decode_sum(shares)
    store_code(share, back / totals, totals)


def total_call(shares, after=()):
    return call(total_kernel, "student_totals", shape(shares[0].shape, I16), after=after, flops=10**6)(*shares)


def last_kernel(share, count, block, place, plan, unit_protos, *refs):
    sum_refs, refs = refs[:count], refs[count:]
    outs, (row_scale, scaled, mixed) = refs[:-3], refs[-3:]
    own = scaled.shape[0]
    width, columns = unit_protos.shape
    scale_rows(sum_refs, row_scale)
    for start in range(0, columns, block):
        here = slice(start, start + block)
        total = None
        for group in range(start, start + block, LANES):
            terms = plan[:own, group : group + LANES] * column_scale(plan, row_scale, group)
            total = terms if total is None else total + terms
            scaled[:, group - start : group - start + LANES] = terms.astype(BF16)
        sides = dot_t(scaled[...], unit_protos[:, here])
        if start == 0:
            mixed[:, width:] = total
            mixed[:, :width] = sides
        else:
            mixed[:, width:] += total
            mixed[:, :width] += sides
    for k, out in enumerate(outs):
        first = pl.multiple_of(jnp.bitwise_xor(place[0], k) * share, share)
        out[...] = mixed[pl.ds(first, share), :]


def last_call(place, plan, unit_protos, sums, own, count, block, after=()):
    rows = plan.shape[0]
    width = unit_protos.shape[0]
    share = own // count
    return call(
        functools.partial(last_kernel, share, len(sums), block),
        "last_sweep",
        [shape((share, width + LANES))] * count,
        [
            pltpu.VMEM((rows, LANES), F32),
            pltpu.VMEM((own, block), BF16),
            pltpu.VMEM((own, width + LANES), F32),
        ],
        scalars=1,
        after=after,
        flops=10**10,
    )(place, plan, unit_protos, *sums)


def as_column(row):
    return jnp.broadcast_to(row, (LANES, row.shape[1])).T[:, :1]


def lane_sums(values):
    return jnp.sum(values, axis=1, keepdims=True)


def code_kernel(*refs):
    parts, out = refs[:-1], refs[-1]
    width = out.shape[1]
    total = tree_sum([part[...] for part in parts])
    store_code(out, total[:, :width], lane_sums(total[:, width:]))


def code_call(parts, after=()):
    rows, columns = parts[0].shape
    out = shape((rows + ROW_TILE, columns - LANES), I16)
    return call(code_kernel, "code_mixed", out, after=after)(*parts)


def gate_call(arrays, after):
    out = call(
        lambda *refs: None,
        "gate",
        [shape(array.shape, array.dtype) for array in arrays],
        after=after,
        aliases={i: i for i in range(len(arrays))},
    )(*arrays)
    return list(out)


def mean_kernel(*refs):
    parts, out = refs[:-1], refs[-1]
    mixed, totals = decode_sum(parts)
    out[...] = mixed / totals


def mean_call(parts, after=()):
    rows, width = parts[0].shape
    return call(mean_kernel, "mean_protos", shape((rows - ROW_TILE, width)), after=after)(*parts)


FIELDS = 4


def prepare_kernel(place, feats, picked, weights, *refs):
    shares, (base, fields, expected, totals) = refs[:-4], refs[-4:]
    rows = shares[0].shape[0] - ROW_TILE
    for k, part in enumerate(shares):
        first = pl.multiple_of(jnp.bitwise_xor(place[0], k) * rows, rows)
        values, extra = decode(part)
        expected[pl.ds(first, rows), :] = values
        totals[pl.ds(first, rows), :] = jnp.broadcast_to(extra, (rows, LANES))
    images = feats.shape[1]
    lane = lax.broadcasted_iota(jnp.int32, (images, LANES), 1)
    for crop in range(feats.shape[0]):
        here = slice(crop * images, (crop + 1) * images)
        raw = feats[crop].astype(F32)
        scales = lax.rsqrt(lane_sums(raw * raw) + epsilon)
        factor = as_column(weights[crop : crop + 1, :].astype(F32)) * (scales * (1.0 / student_softness))
        cubic = factor * scales * scales
        mean = expected[here, :]
        base[here, :] = factor * mean - (cubic * lane_sums(raw * mean)) * raw
        logs = jnp.log(totals[here, :])
        view = as_column(picked[crop : crop + 1, :].astype(F32))
        fields[here, :] = jnp.where(
            lane == 0, factor, jnp.where(lane == 1, cubic, jnp.where(lane == 2, scales, logs))
        )
        fields[here, :] = jnp.where(lane == FIELDS, view, fields[here, :])


def prepare_call(place, feats, picked, weights, shares, after=()):
    crops, images, width = feats.shape
    rows = crops * images
    return call(
        prepare_kernel,
        "prepare",
        [shape((rows, width)), shape((rows, LANES))],
        [pltpu.VMEM((rows, width), F32), pltpu.VMEM((rows, LANES), F32)],
        scalars=1,
        after=after,
    )(place, feats, picked, weights, *shares)


def finish_kernel(views, place, feats, base, fields, *refs):
    parts, (gradient, loss, means) = refs[:-3], refs[-3:]
    rows = parts[0].shape[0]
    for k, part in enumerate(parts):
        first = pl.multiple_of(jnp.bitwise_xor(place[0], k) * rows, rows)
        means[pl.ds(first, rows), :] = part[...]
    images = feats.shape[1]
    for crop in range(feats.shape[0]):
        here = slice(crop * images, (crop + 1) * images)
        raw = feats[crop].astype(F32)
        factor, cubic, scales = (fields[here, k : k + 1] for k in range(3))
        view_column = fields[here, FIELDS : FIELDS + 1]
        chosen = means[:images, :]
        for view in range(1, views):
            chosen = jnp.where(view_column == view, means[view * images : (view + 1) * images, :], chosen)
        along = cubic * lane_sums(raw * chosen)
        gradient[crop] = base[here, :] - factor * chosen + along * raw
        unit = (raw * scales).astype(BF16).astype(F32)
        column = fields[here, FIELDS - 1 : FIELDS] - lane_sums(unit * chosen) * (1.0 / student_softness)
        loss[crop : crop + 1, :] = jnp.broadcast_to(column, (images, LANES)).T[:1, :]


def finish_call(views, place, feats, base, fields, means):
    crops, images, width = feats.shape
    return call(
        functools.partial(finish_kernel, views),
        "finish",
        [shape((crops, images, width)), shape((crops, images))],
        [pltpu.VMEM((views * images, width), F32)],
        scalars=1,
    )(place, feats, base, fields, *means)


def shards(teacher_feats, student_feats, teacher_protos, student_protos, pairing, row_weight):
    images, views, width = teacher_feats.shape
    crops = student_feats.shape[0]
    image_devices = lax.axis_size("image")
    crop_devices = lax.axis_size("crop")
    proto_devices = lax.axis_size("proto")
    crop_place = lax.axis_index("crop").reshape(1)
    proto_place = lax.axis_index("proto").reshape(1)
    block = 512

    teacher_parts = [teacher_feats] + [swap(teacher_feats, "image", k) for k in range(1, image_devices)]
    feats = student_feats.reshape(crops * images, width)
    protos = [student_protos] + [swap(student_protos, "crop", k) for k in range(1, crop_devices)]

    pieces = proto_devices
    if crops * images % (proto_devices * ROW_TILE):
        pieces, proto_place = 1, jnp.zeros((1,), jnp.int32)
    few = crop_devices * proto_devices <= 8
    copies = 1 if few else crop_devices * proto_devices

    def from_all(shares):
        return [shares[0]] + [swap(shares[k % len(shares)], "proto", k) for k in range(1, proto_devices)]

    def exchange(sums, shares):
        if not few:
            return [lax.all_to_all(sums, ("crop", "proto"), 0, 0)], shares
        total, shares = join_call([sums] + [swap(sums, "crop", k) for k in range(1, crop_devices)], shares)
        return from_all([total]), shares

    unit_protos, unit_teacher, unit_feats, back = own_call(
        crop_place, proto_place, feats, student_protos, teacher_protos, block
    )
    shares = other_call(proto_place, unit_feats, back, protos[1:], pieces, block)
    plan, sums = first_call(teacher_parts, unit_teacher, copies, block)
    row_sums, shares = exchange(sums, shares)
    shares = from_all(shares)
    sums, plan = sweep_call(plan, copies, row_sums)
    row_sums, shares = exchange(sums, [total_call(shares, after=[sums])])
    shares = [shares[0]] + [swap(shares[0], "proto", k) for k in range(1, pieces)]
    mixed = last_call(
        crop_place,
        plan,
        unit_protos,
        row_sums,
        views * images,
        crop_devices,
        block,
    )
    mixed = [mixed[0]] + gate_call(mixed[1:], shares[1:])

    coded = code_call([mixed[0]] + [swap(mixed[k], "crop", k) for k in range(1, crop_devices)])
    base, fields = prepare_call(proto_place, student_feats, pairing, row_weight, shares, after=[coded])
    means = mean_call(from_all([coded]), after=[base])
    means = [means] + [swap(means, "crop", k) for k in range(1, crop_devices)]
    return finish_call(views, crop_place, student_feats, base, fields, means)


def solution(mesh):
    in_specs = (
        P("image", None, None),
        P("crop", "image", None),
        P(None, ("crop", "proto")),
        P(None, ("crop", "proto")),
        P("crop", "image"),
        P("crop", "image"),
    )
    out_specs = (P("crop", "image", None), P("crop", "image"))
    return jax.shard_map(shards, mesh=mesh, in_specs=in_specs, out_specs=out_specs, check_vma=False)
```

```python
import functools

import jax
import jax.numpy as jnp
from jax import lax
from jax.experimental import pallas as pl
from jax.experimental.pallas import tpu as pltpu
from jax.sharding import PartitionSpec as P

SWEEPS = 3
LANES = 128
ROW_TILE = 16
LEVELS = 32767.0
PARTS = 32768.0

epsilon = 1e-06
student_softness = 0.1
teacher_softness = 0.04

F32 = jnp.float32
BF16 = jnp.bfloat16
I16 = jnp.int16

IN_VMEM = pl.BlockSpec(memory_space=pltpu.VMEM)
IN_HBM = pl.BlockSpec(memory_space=pltpu.HBM)
IN_SMEM = pl.BlockSpec(memory_space=pltpu.SMEM)


def call(kernel, name, out_shape, scratch=(), scalars=0, vmem=16, after=(), flops=10**9, aliases=None, far=()):
    def run(*operands):
        count = len(operands)

        def body(*refs):
            kernel(*refs[:count], *refs[count + len(after) :])

        return pl.pallas_call(
            body,
            in_specs=[IN_SMEM] * scalars
            + [IN_HBM if i in far else IN_VMEM for i in range(scalars, count)]
            + [pl.BlockSpec(memory_space=pl.ANY)] * len(after),
            out_specs=jax.tree.map(lambda _: IN_VMEM, out_shape),
            out_shape=out_shape,
            scratch_shapes=list(scratch),
            compiler_params=pltpu.CompilerParams(vmem_limit_bytes=vmem * 1024 * 1024),
            cost_estimate=pl.CostEstimate(flops=flops, bytes_accessed=0, transcendentals=0),
            input_output_aliases=aliases or {},
            name=name,
        )(*operands, *after)

    return run


def shape(dims, dtype=F32):
    return jax.ShapeDtypeStruct(dims, dtype)


def unit_rows(raw_rows):
    return raw_rows * lax.rsqrt(jnp.sum(raw_rows * raw_rows, axis=-1, keepdims=True) + epsilon)


def unit_columns(entries):
    return entries * lax.rsqrt(jnp.sum(entries * entries, axis=0, keepdims=True) + epsilon)


def lane_groups(values):
    total = values[:, :LANES]
    for start in range(LANES, values.shape[1], LANES):
        total = total + values[:, start : start + LANES]
    return total


def dot_t(a, b):
    return lax.dot_general(a, b, (((1,), (1,)), ((), ())), preferred_element_type=F32)


def row_vector(partial):
    return jnp.sum(partial.T, axis=0, keepdims=True)


def tree_sum(terms):
    while len(terms) > 1:
        terms = [terms[i] + terms[i + 1] for i in range(0, len(terms), 2)]
    return terms[0]


def split_positive(values):
    power = jnp.floor(jnp.log2(jnp.maximum(values, 1e-30))) + 1.0
    scaled = values * jnp.exp2(-power) * PARTS
    high = jnp.minimum(jnp.floor(scaled), LEVELS)
    low = jnp.minimum(jnp.floor((scaled - high) * PARTS), LEVELS)
    return power, high, low


def join_positive(power, high, low):
    return (high + low * (1.0 / PARTS)) * (1.0 / PARTS) * jnp.exp2(power)


def to_i16(values):
    return values.astype(jnp.int32).astype(I16)


def to_f32(values):
    return values.astype(jnp.int32).astype(F32)


def coded(rows, width):
    return jax.ShapeDtypeStruct((rows * width // LANES + ROW_TILE, LANES), I16)


def store_code(out, values, extra):
    rows, width = values.shape
    largest = jnp.maximum(jnp.max(jnp.abs(values), axis=1, keepdims=True), 1e-30)
    power = jnp.floor(jnp.log2(largest)) + 1.0
    whole = jnp.floor(values * (jnp.exp2(-power) * LEVELS) + 0.5)
    whole = to_i16(jnp.clip(whole, -LEVELS, LEVELS))
    for k in range(width // LANES):
        out[k * rows : (k + 1) * rows, :] = whole[:, k * LANES : (k + 1) * LANES]
    extra_power, high, low = split_positive(extra)
    lane = lax.broadcasted_iota(jnp.int32, (rows, LANES), 1)
    tail = jnp.where(lane == 0, power, jnp.where(lane == 1, extra_power, jnp.where(lane == 2, high, low)))
    if rows < LANES:
        tail = jnp.concatenate([tail, jnp.zeros((LANES - rows, LANES), F32)], axis=0)
    out[out.shape[0] - ROW_TILE :, :] = to_i16(tail.T[:ROW_TILE, :])


def decode(ref, rows):
    count = (ref.shape[0] - ROW_TILE) // rows
    block = to_f32(ref[count * rows :, :])
    tail = jnp.concatenate([block, jnp.zeros((LANES - ROW_TILE, LANES), F32)], axis=0).T[:rows, :]
    values = jnp.concatenate([to_f32(ref[k * rows : (k + 1) * rows, :]) for k in range(count)], axis=1)
    values = values * (jnp.exp2(tail[:, 0:1]) * (1.0 / LEVELS))
    return values, join_positive(tail[:, 1:2], tail[:, 2:3], tail[:, 3:4])


def decode_sum(refs, rows):
    pairs = [decode(ref, rows) for ref in refs]
    return tree_sum([p[0] for p in pairs]), tree_sum([p[1] for p in pairs])


SUMS_AT = 4


def pack_kernel(count, *refs):
    parts, refs = refs[:count], refs[count:]
    shares, outs = refs[: len(refs) // 2], refs[len(refs) // 2 :]
    terms = split_positive(tree_sum([part[0] for part in parts]))
    groups = terms[0].shape[1] // LANES
    for share, out in zip(shares, outs):
        last = share.shape[0] - ROW_TILE
        out[:last, :] = share[:last, :]
        at = lax.broadcasted_iota(jnp.int32, (ROW_TILE, LANES), 0)
        under = to_f32(share[last:, :])
        for k, row in enumerate(terms):
            for j in range(groups):
                piece = row[:, j * LANES : (j + 1) * LANES]
                under = jnp.where(at == SUMS_AT + k * groups + j, piece, under)
        out[last:, :] = to_i16(under)


def pack_call(parts, shares):
    return call(
        functools.partial(pack_kernel, len(parts)),
        "pack_sums",
        [shape(share.shape, I16) for share in shares],
    )(*parts, *shares)


def read_sums(refs):
    if refs[0].dtype == I16:
        terms = []
        groups = (ROW_TILE - SUMS_AT) // 3
        for ref in refs:
            under = to_f32(ref[ref.shape[0] - ROW_TILE :, :])
            rows = [
                jnp.concatenate([under[at + j : at + j + 1, :] for j in range(groups)], axis=1)
                for at in range(SUMS_AT, SUMS_AT + 3 * groups, groups)
            ]
            terms.append(join_positive(*rows))
        return tree_sum(terms)
    total = refs[0][0]
    for k in range(1, refs[0].shape[0]):
        total = total + refs[0][k]
    return total


def swap(values, axis, distance):
    count = lax.axis_size(axis)
    return lax.ppermute(values, axis, [(i, i ^ distance) for i in range(count)])


def fetch(sources, buffers, sems, block):
    columns = buffers[0].shape[1]
    copies = []
    for j, start in enumerate(range(0, columns, block)):
        here = pl.ds(start, block)
        copies.append(
            [
                pltpu.make_async_copy(source.at[:, here], buffer.at[:, here], sems.at[i, j])
                for i, (source, buffer) in enumerate(zip(sources, buffers))
            ]
        )
    for group in copies:
        for copy in group:
            copy.start()
    return copies


def add_side(back, unit_feats, weights, fresh):
    width = weights.shape[0]
    logits = jnp.dot(unit_feats[...], weights, preferred_element_type=F32)
    terms = jnp.exp(logits * (1.0 / student_softness))
    sums = lane_groups(terms)
    sides = dot_t(terms.astype(BF16), weights)
    if fresh:
        back[:, width:] = sums
        back[:, :width] = sides
    else:
        back[:, width:] += sums
        back[:, :width] += sides


def own_kernel(block, crop_place, proto_place, feats, protos, teacher_protos, unit_protos, unit_teacher, unit_feats, back, *refs):
    raw, buffers, raw_sem, sems = refs[0], refs[1:3], refs[3], refs[4]
    raw_copy = pltpu.make_async_copy(feats, raw, raw_sem)
    raw_copy.start()
    copies = fetch([protos, teacher_protos], buffers, sems, block)
    raw_copy.wait()
    unit_feats[...] = unit_rows(raw[...].astype(F32)).astype(BF16)
    for j, group in enumerate(copies):
        here = slice(j * block, (j + 1) * block)
        group[0].wait()
        weights = unit_columns(buffers[0][:, here].astype(F32)).astype(BF16)
        unit_protos[:, here] = weights
        add_side(back, unit_feats, weights, j == 0)
        group[1].wait()
        unit_teacher[:, here] = unit_columns(buffers[1][:, here].astype(F32)).astype(BF16)


def own_call(crop_place, proto_place, feats, protos, teacher_protos, block):
    width, columns = protos.shape
    rows = feats.shape[0]
    return call(
        functools.partial(own_kernel, block),
        "student_own",
        [shape((width, columns), BF16)] * 2 + [shape((rows, width), BF16), shape((rows, width + LANES))],
        [pltpu.VMEM((rows, width), BF16)]
        + [pltpu.VMEM((width, columns), BF16)] * 2
        + [pltpu.SemaphoreType.DMA, pltpu.SemaphoreType.DMA((2, columns // block))],
        scalars=2,
        vmem=47,
        far=[2, 3, 4],
        flops=4 * rows * columns * width,
    )(crop_place, proto_place, feats, protos, teacher_protos)


def other_kernel(count, block, place, unit_feats, partial, *refs):
    sources, refs = refs[:count], refs[count:]
    outs, refs = refs[: -count - 2], refs[-count - 2 :]
    back, buffers, sems = refs[0], refs[1:-1], refs[-1]
    width = unit_feats.shape[1]
    copies = fetch(sources, buffers, sems, block)
    back[...] = partial[...]
    for j, group in enumerate(copies):
        here = slice(j * block, (j + 1) * block)
        for copy, buffer in zip(group, buffers):
            copy.wait()
            weights = unit_columns(buffer[:, here].astype(F32)).astype(BF16)
            add_side(back, unit_feats, weights, False)
    share = back.shape[0] // len(outs)
    for k, out in enumerate(outs):
        first = pl.multiple_of(jnp.bitwise_xor(place[0], k) * share, share)
        total = back[pl.ds(first, share), :]
        store_code(out, total[:, :width], lane_sums(total[:, width:]))


def other_call(place, unit_feats, back, protos, pieces, block):
    width, columns = protos[0].shape
    rows = unit_feats.shape[0]
    count = len(protos)
    return call(
        functools.partial(other_kernel, count, block),
        "student_other",
        [coded(rows // pieces, width)] * pieces,
        [pltpu.VMEM((rows, width + LANES), F32)]
        + [pltpu.VMEM((width, columns), BF16)] * count
        + [pltpu.SemaphoreType.DMA((count, columns // block))],
        scalars=1,
        vmem=48 if count > 1 else 16,
        far=range(3, 3 + count),
        flops=4 * rows * count * columns * width,
    )(place, unit_feats, back, *protos)


def first_kernel(count, block, *refs):
    parts, (weights, plan, sums, unit, partial) = refs[:count], refs[count:]
    columns = weights.shape[1]
    first = 0
    for part in parts:
        images, views, _ = part.shape
        for view in range(views):
            unit[first : first + images, :] = unit_rows(part[:, view, :].astype(F32)).astype(BF16)
            first += images
    for start in range(0, columns, block):
        here = slice(start, start + block)
        column_sums = None
        for first in range(0, unit.shape[0], LANES):
            values = jnp.exp(
                jnp.dot(unit[first : first + LANES, :], weights[:, here], preferred_element_type=F32)
                * (1.0 / teacher_softness)
            )
            plan[first : first + LANES, here] = values
            total = jnp.sum(values, axis=0, keepdims=True)
            column_sums = total if column_sums is None else column_sums + total
        terms = lane_groups(plan[:, here] * (1.0 / column_sums))
        if start == 0:
            partial[...] = terms
        else:
            partial[...] += terms
    store_sums(sums, partial)


def store_sums(sums, partial):
    total = row_vector(partial[...])
    for k in range(sums.shape[0]):
        sums[k] = total


def first_call(parts, weights, copies, block, after=()):
    columns = weights.shape[1]
    rows = sum(part.shape[0] * part.shape[1] for part in parts)
    return call(
        functools.partial(first_kernel, len(parts), block),
        "first_sweep",
        [shape((rows, columns)), shape((copies, 1, rows))],
        [pltpu.VMEM((rows, weights.shape[0]), BF16), pltpu.VMEM((rows, LANES), F32)],
        after=after,
        flops=8 * rows * columns * weights.shape[0],
    )(*parts, weights)


def scale_rows(sum_refs, row_scale):
    scale = 1.0 / read_sums(sum_refs)
    row_scale[...] = jnp.broadcast_to(scale, (LANES, scale.shape[1])).T


def column_scale(plan, row_scale, start):
    weighted = plan[:, start : start + LANES] * row_scale[...]
    return 1.0 / jnp.sum(weighted, axis=0, keepdims=True)


def sweep_kernel(count, share_rows, plan, *refs):
    shares, refs = refs[:count], refs[count:]
    sum_refs, (sums, share, _, row_scale, partial) = refs[:-5] or shares, refs[-5:]
    scale_rows(sum_refs, row_scale)
    for start in range(0, plan.shape[1], LANES):
        terms = plan[:, start : start + LANES] * column_scale(plan, row_scale, start)
        if start == 0:
            partial[...] = terms
        else:
            partial[...] += terms
    store_sums(sums, partial)
    back, totals = decode_sum(shares, share_rows)
    store_code(share, back / totals, totals)


def sweep_call(plan, copies, share_rows, shares, row_sums):
    rows = plan.shape[0]
    return call(
        functools.partial(sweep_kernel, len(shares), share_rows),
        "sweep",
        [shape((copies, 1, rows)), shape(shares[0].shape, I16), shape(plan.shape)],
        [pltpu.VMEM((rows, LANES), F32)] * 2,
        aliases={0: 2},
    )(plan, *shares, *row_sums)


def last_kernel(share, count, block, place, plan, unit_protos, *refs):
    sum_refs, refs = refs[:count], refs[count:]
    outs, (row_scale, scaled, mixed) = refs[:-3], refs[-3:]
    own = scaled.shape[0]
    width, columns = unit_protos.shape
    scale_rows(sum_refs, row_scale)
    for start in range(0, columns, block):
        here = slice(start, start + block)
        total = None
        for group in range(start, start + block, LANES):
            terms = plan[:own, group : group + LANES] * column_scale(plan, row_scale, group)
            total = terms if total is None else total + terms
            scaled[:, group - start : group - start + LANES] = terms.astype(BF16)
        sides = dot_t(scaled[...], unit_protos[:, here])
        if start == 0:
            mixed[:, width:] = total
            mixed[:, :width] = sides
        else:
            mixed[:, width:] += total
            mixed[:, :width] += sides
    for k, out in enumerate(outs):
        first = pl.multiple_of(jnp.bitwise_xor(place[0], k) * share, share)
        out[...] = mixed[pl.ds(first, share), :]


def last_call(place, plan, unit_protos, sums, own, count, block, after=()):
    rows = plan.shape[0]
    width = unit_protos.shape[0]
    share = own // count
    return call(
        functools.partial(last_kernel, share, len(sums), block),
        "last_sweep",
        [shape((share, width + LANES))] * count,
        [
            pltpu.VMEM((rows, LANES), F32),
            pltpu.VMEM((own, block), BF16),
            pltpu.VMEM((own, width + LANES), F32),
        ],
        scalars=1,
        after=after,
    )(place, plan, unit_protos, *sums)


def as_column(row):
    return jnp.broadcast_to(row, (LANES, row.shape[1])).T[:, :1]


def lane_sums(values):
    return jnp.sum(values, axis=1, keepdims=True)


def code_kernel(*refs):
    parts, out = refs[:-1], refs[-1]
    width = parts[0].shape[1] - LANES
    total = tree_sum([part[...] for part in parts])
    store_code(out, total[:, :width], lane_sums(total[:, width:]))


def code_call(parts, after=()):
    rows, columns = parts[0].shape
    out = coded(rows, columns - LANES)
    return call(code_kernel, "code_mixed", out, after=after)(*parts)


def mean_kernel(*refs):
    parts, out = refs[:-1], refs[-1]
    mixed, totals = decode_sum(parts, out.shape[0])
    out[...] = mixed / totals


def mean_call(parts, width, after=()):
    rows = (parts[0].shape[0] - ROW_TILE) * LANES // width
    return call(mean_kernel, "mean_protos", shape((rows, width)), after=after)(*parts)


FIELDS = 4


def prepare_kernel(place, feats, picked, weights, *refs):
    shares, (base, fields, expected, totals) = refs[:-4], refs[-4:]
    rows = expected.shape[0] // len(shares)
    for k, part in enumerate(shares):
        first = pl.multiple_of(jnp.bitwise_xor(place[0], k) * rows, rows)
        values, extra = decode(part, rows)
        expected[pl.ds(first, rows), :] = values
        totals[pl.ds(first, rows), :] = jnp.broadcast_to(extra, (rows, LANES))
    images = feats.shape[1]
    lane = lax.broadcasted_iota(jnp.int32, (images, LANES), 1)
    for crop in range(feats.shape[0]):
        here = slice(crop * images, (crop + 1) * images)
        raw = feats[crop].astype(F32)
        scales = lax.rsqrt(lane_sums(raw * raw) + epsilon)
        factor = as_column(weights[crop : crop + 1, :].astype(F32)) * (scales * (1.0 / student_softness))
        cubic = factor * scales * scales
        mean = expected[here, :]
        base[here, :] = factor * mean - (cubic * lane_sums(raw * mean)) * raw
        logs = jnp.log(totals[here, :])
        view = as_column(picked[crop : crop + 1, :].astype(F32))
        fields[here, :] = jnp.where(
            lane == 0, factor, jnp.where(lane == 1, cubic, jnp.where(lane == 2, scales, logs))
        )
        fields[here, :] = jnp.where(lane == FIELDS, view, fields[here, :])


def prepare_call(place, feats, picked, weights, shares, after=()):
    crops, images, width = feats.shape
    rows = crops * images
    return call(
        prepare_kernel,
        "prepare",
        [shape((rows, width)), shape((rows, LANES))],
        [pltpu.VMEM((rows, width), F32), pltpu.VMEM((rows, LANES), F32)],
        scalars=1,
        after=after,
    )(place, feats, picked, weights, *shares)


def finish_kernel(views, place, feats, base, fields, *refs):
    parts, (gradient, loss, means) = refs[:-3], refs[-3:]
    rows = parts[0].shape[0]
    for k, part in enumerate(parts):
        first = pl.multiple_of(jnp.bitwise_xor(place[0], k) * rows, rows)
        means[pl.ds(first, rows), :] = part[...]
    images = feats.shape[1]
    for crop in range(feats.shape[0]):
        here = slice(crop * images, (crop + 1) * images)
        raw = feats[crop].astype(F32)
        factor, cubic, scales = (fields[here, k : k + 1] for k in range(3))
        view_column = fields[here, FIELDS : FIELDS + 1]
        chosen = means[:images, :]
        for view in range(1, views):
            chosen = jnp.where(view_column == view, means[view * images : (view + 1) * images, :], chosen)
        along = cubic * lane_sums(raw * chosen)
        gradient[crop] = base[here, :] - factor * chosen + along * raw
        unit = (raw * scales).astype(BF16).astype(F32)
        column = fields[here, FIELDS - 1 : FIELDS] - lane_sums(unit * chosen) * (1.0 / student_softness)
        loss[crop : crop + 1, :] = jnp.broadcast_to(column, (images, LANES)).T[:1, :]


def finish_call(views, place, feats, base, fields, means):
    crops, images, width = feats.shape
    return call(
        functools.partial(finish_kernel, views),
        "finish",
        [shape((crops, images, width)), shape((crops, images))],
        [pltpu.VMEM((views * images, width), F32)],
        scalars=1,
    )(place, feats, base, fields, *means)


def shards(teacher_feats, student_feats, teacher_protos, student_protos, pairing, row_weight):
    images, views, width = teacher_feats.shape
    crops = student_feats.shape[0]
    image_devices = lax.axis_size("image")
    crop_devices = lax.axis_size("crop")
    proto_devices = lax.axis_size("proto")
    crop_place = lax.axis_index("crop").reshape(1)
    proto_place = lax.axis_index("proto").reshape(1)
    block = 512

    teacher_parts = [teacher_feats] + [swap(teacher_feats, "image", k) for k in range(1, image_devices)]
    feats = student_feats.reshape(crops * images, width)
    protos = [student_protos] + [swap(student_protos, "crop", k) for k in range(1, crop_devices)]

    teacher_rows = image_devices * images * views
    joint = crops * images % (proto_devices * ROW_TILE) == 0 and 3 * teacher_rows == (ROW_TILE - SUMS_AT) * LANES
    pieces, copies = (proto_devices, 1) if joint else (1, crop_devices * proto_devices)
    if not joint:
        proto_place = jnp.zeros((1,), jnp.int32)

    def from_all(shares):
        return [shares[0]] + [swap(shares[k % len(shares)], "proto", k) for k in range(1, proto_devices)]

    def exchange(sums, shares):
        if joint:
            parts = [sums] + [swap(sums, "crop", k) for k in range(1, crop_devices)]
            return from_all(pack_call(parts, shares)), []
        return from_all(shares), [lax.all_to_all(sums, ("crop", "proto"), 0, 0)]

    unit_protos, unit_teacher, unit_feats, back = own_call(
        crop_place, proto_place, feats, student_protos, teacher_protos, block
    )
    shares = other_call(proto_place, unit_feats, back, protos[1:], pieces, block)
    plan, sums = first_call(teacher_parts, unit_teacher, copies, block)
    for _ in range(SWEEPS - 2):
        shares, row_sums = exchange(sums, shares)
        sums, share, plan = sweep_call(plan, copies, crops * images // pieces, shares, row_sums)
        shares = [share]
    if joint:
        shares, row_sums = exchange(sums, shares)
    else:
        row_sums = [lax.all_to_all(sums, ("crop", "proto"), 0, 0)]
    mixed = last_call(
        crop_place, plan, unit_protos, row_sums or shares, views * images, crop_devices, block
    )

    sent = code_call([mixed[0]] + [swap(mixed[k], "crop", k) for k in range(1, crop_devices)])
    base, fields = prepare_call(proto_place, student_feats, pairing, row_weight, shares, after=[sent])
    means = mean_call(from_all([sent]), width, after=[base])
    means = [means] + [swap(means, "crop", k) for k in range(1, crop_devices)]
    return finish_call(views, crop_place, student_feats, base, fields, means)


def solution(mesh):
    in_specs = (
        P("image", None, None),
        P("crop", "image", None),
        P(None, ("crop", "proto")),
        P(None, ("crop", "proto")),
        P("crop", "image"),
        P("crop", "image"),
    )
    out_specs = (P("crop", "image", None), P("crop", "image"))
    return jax.shard_map(shards, mesh=mesh, in_specs=in_specs, out_specs=out_specs, check_vma=False)
```

```python
import functools

import jax
import jax.numpy as jnp
from jax import lax
from jax.experimental import pallas as pl
from jax.experimental.pallas import tpu as pltpu
from jax.sharding import PartitionSpec as P

SWEEPS = 3
LANES = 128
ROW_TILE = 16
LEVELS = 32767.0
PARTS = 32768.0

epsilon = 1e-06
student_softness = 0.1
teacher_softness = 0.04

F32 = jnp.float32
BF16 = jnp.bfloat16
I16 = jnp.int16

IN_VMEM = pl.BlockSpec(memory_space=pltpu.VMEM)
IN_HBM = pl.BlockSpec(memory_space=pltpu.HBM)
IN_SMEM = pl.BlockSpec(memory_space=pltpu.SMEM)


def call(kernel, name, out_shape, scratch=(), scalars=0, vmem=16, after=(), flops=10**9, aliases=None, far=(), far_out=()):
    def run(*operands):
        count = len(operands)

        def body(*refs):
            kernel(*refs[:count], *refs[count + len(after) :])

        return pl.pallas_call(
            body,
            in_specs=[IN_SMEM] * scalars
            + [IN_HBM if i in far else IN_VMEM for i in range(scalars, count)]
            + [pl.BlockSpec(memory_space=pl.ANY)] * len(after),
            out_specs=[IN_HBM if i in far_out else IN_VMEM for i in range(len(out_shape))]
            if isinstance(out_shape, list)
            else IN_VMEM,
            out_shape=out_shape,
            scratch_shapes=list(scratch),
            compiler_params=pltpu.CompilerParams(vmem_limit_bytes=vmem * 1024 * 1024),
            cost_estimate=pl.CostEstimate(flops=flops, bytes_accessed=0, transcendentals=0),
            input_output_aliases=aliases or {},
            name=name,
        )(*operands, *after)

    return run


def shape(dims, dtype=F32):
    return jax.ShapeDtypeStruct(dims, dtype)


def unit_rows(raw_rows):
    return raw_rows * lax.rsqrt(jnp.sum(raw_rows * raw_rows, axis=-1, keepdims=True) + epsilon)


def unit_columns(entries):
    return entries * lax.rsqrt(jnp.sum(entries * entries, axis=0, keepdims=True) + epsilon)


def lane_groups(values):
    total = values[:, :LANES]
    for start in range(LANES, values.shape[1], LANES):
        total = total + values[:, start : start + LANES]
    return total


def dot_t(a, b):
    return lax.dot_general(a, b, (((1,), (1,)), ((), ())), preferred_element_type=F32)


def row_vector(partial):
    return jnp.sum(partial.T, axis=0, keepdims=True)


def tree_sum(terms):
    while len(terms) > 1:
        terms = [terms[i] + terms[i + 1] for i in range(0, len(terms), 2)]
    return terms[0]


def split_positive(values):
    power = jnp.floor(jnp.log2(jnp.maximum(values, 1e-30))) + 1.0
    scaled = values * jnp.exp2(-power) * PARTS
    high = jnp.minimum(jnp.floor(scaled), LEVELS)
    low = jnp.minimum(jnp.floor((scaled - high) * PARTS), LEVELS)
    return power, high, low


def join_positive(power, high, low):
    return (high + low * (1.0 / PARTS)) * (1.0 / PARTS) * jnp.exp2(power)


def to_i16(values):
    return values.astype(jnp.int32).astype(I16)


def to_f32(values):
    return values.astype(jnp.int32).astype(F32)


def coded(rows, width):
    return jax.ShapeDtypeStruct((rows * width // LANES + ROW_TILE, LANES), I16)


def store_code(out, values, extra):
    rows, width = values.shape
    largest = jnp.maximum(jnp.max(jnp.abs(values), axis=1, keepdims=True), 1e-30)
    power = jnp.floor(jnp.log2(largest)) + 1.0
    whole = jnp.floor(values * (jnp.exp2(-power) * LEVELS) + 0.5)
    whole = to_i16(jnp.clip(whole, -LEVELS, LEVELS))
    for k in range(width // LANES):
        out[k * rows : (k + 1) * rows, :] = whole[:, k * LANES : (k + 1) * LANES]
    extra_power, high, low = split_positive(extra)
    lane = lax.broadcasted_iota(jnp.int32, (rows, LANES), 1)
    tail = jnp.where(lane == 0, power, jnp.where(lane == 1, extra_power, jnp.where(lane == 2, high, low)))
    if rows < LANES:
        tail = jnp.concatenate([tail, jnp.zeros((LANES - rows, LANES), F32)], axis=0)
    out[out.shape[0] - ROW_TILE :, :] = to_i16(tail.T[:ROW_TILE, :])


def decode(ref, rows):
    count = (ref.shape[0] - ROW_TILE) // rows
    block = to_f32(ref[count * rows :, :])
    tail = jnp.concatenate([block, jnp.zeros((LANES - ROW_TILE, LANES), F32)], axis=0).T[:rows, :]
    values = jnp.concatenate([to_f32(ref[k * rows : (k + 1) * rows, :]) for k in range(count)], axis=1)
    values = values * (jnp.exp2(tail[:, 0:1]) * (1.0 / LEVELS))
    return values, join_positive(tail[:, 1:2], tail[:, 2:3], tail[:, 3:4])


def decode_sum(refs, rows):
    pairs = [decode(ref, rows) for ref in refs]
    return tree_sum([p[0] for p in pairs]), tree_sum([p[1] for p in pairs])


SUMS_AT = 4


def pack_kernel(count, *refs):
    parts, refs = refs[:count], refs[count:]
    shares, outs = refs[: len(refs) // 2], refs[len(refs) // 2 :]
    terms = split_positive(tree_sum([part[0] for part in parts]))
    groups = terms[0].shape[1] // LANES
    for share, out in zip(shares, outs):
        last = share.shape[0] - ROW_TILE
        out[:last, :] = share[:last, :]
        at = lax.broadcasted_iota(jnp.int32, (ROW_TILE, LANES), 0)
        under = to_f32(share[last:, :])
        for k, row in enumerate(terms):
            for j in range(groups):
                piece = row[:, j * LANES : (j + 1) * LANES]
                under = jnp.where(at == SUMS_AT + k * groups + j, piece, under)
        out[last:, :] = to_i16(under)


def pack_call(parts, shares):
    return call(
        functools.partial(pack_kernel, len(parts)),
        "pack_sums",
        [shape(share.shape, I16) for share in shares],
    )(*parts, *shares)


def read_sums(refs):
    if refs[0].dtype == I16:
        terms = []
        groups = (ROW_TILE - SUMS_AT) // 3
        for ref in refs:
            under = to_f32(ref[ref.shape[0] - ROW_TILE :, :])
            rows = [
                jnp.concatenate([under[at + j : at + j + 1, :] for j in range(groups)], axis=1)
                for at in range(SUMS_AT, SUMS_AT + 3 * groups, groups)
            ]
            terms.append(join_positive(*rows))
        return tree_sum(terms)
    total = refs[0][0]
    for k in range(1, refs[0].shape[0]):
        total = total + refs[0][k]
    return total


def swap(values, axis, distance):
    count = lax.axis_size(axis)
    return lax.ppermute(values, axis, [(i, i ^ distance) for i in range(count)])


def fetch(sources, buffers, sems, block, first=0, last=None):
    last = buffers[0].shape[1] if last is None else last
    copies = []
    for j, start in enumerate(range(first, last, block)):
        here = pl.ds(start, block)
        copies.append(
            [
                pltpu.make_async_copy(source.at[:, here], buffer.at[:, here], sems.at[i, j])
                for i, (source, buffer) in enumerate(zip(sources, buffers))
            ]
        )
    for group in copies:
        for copy in group:
            copy.start()
    return copies


def add_side(back, unit_feats, weights, fresh):
    width = weights.shape[0]
    logits = jnp.dot(unit_feats[...], weights, preferred_element_type=F32)
    terms = jnp.exp(logits * (1.0 / student_softness))
    sums = lane_groups(terms)
    sides = dot_t(terms.astype(BF16), weights)
    if fresh:
        back[:, width:] = sums
        back[:, :width] = sides
    else:
        back[:, width:] += sums
        back[:, :width] += sides


def own_kernel(block, crop_place, proto_place, feats, protos, teacher_protos, unit_protos, unit_teacher, unit_feats, back, *refs):
    raw, buffers, raw_sem, sems = refs[0], refs[1:3], refs[3], refs[4]
    raw_copy = pltpu.make_async_copy(feats, raw, raw_sem)
    raw_copy.start()
    copies = fetch([protos, teacher_protos], buffers, sems, block)
    raw_copy.wait()
    unit_feats[...] = unit_rows(raw[...].astype(F32)).astype(BF16)
    for j, group in enumerate(copies):
        here = slice(j * block, (j + 1) * block)
        group[0].wait()
        weights = unit_columns(buffers[0][:, here].astype(F32)).astype(BF16)
        unit_protos[:, here] = weights
        add_side(back, unit_feats, weights, j == 0)
        group[1].wait()
        unit_teacher[:, here] = unit_columns(buffers[1][:, here].astype(F32)).astype(BF16)


def own_call(crop_place, proto_place, feats, protos, teacher_protos, block):
    width, columns = protos.shape
    rows = feats.shape[0]
    return call(
        functools.partial(own_kernel, block),
        "student_own",
        [shape((width, columns), BF16)] * 2 + [shape((rows, width), BF16), shape((rows, width + LANES))],
        [pltpu.VMEM((rows, width), BF16)]
        + [pltpu.VMEM((width, columns), BF16)] * 2
        + [pltpu.SemaphoreType.DMA, pltpu.SemaphoreType.DMA((2, columns // block))],
        scalars=2,
        vmem=47,
        far=[2, 3, 4],
        flops=4 * rows * columns * width,
    )(crop_place, proto_place, feats, protos, teacher_protos)


def begin_kernel(count, block, last, unit_feats, partial, *refs):
    sources, (back, *buffers, sems) = refs[:count], refs[count:]
    copies = fetch(sources, buffers, sems, block, 0, last)
    back[...] = partial[...]
    add_blocks(copies, buffers, back, unit_feats, block, 0)


def add_blocks(copies, buffers, back, unit_feats, block, first):
    for j, group in enumerate(copies):
        here = slice(first + j * block, first + (j + 1) * block)
        for copy, buffer in zip(group, buffers):
            copy.wait()
            weights = unit_columns(buffer[:, here].astype(F32)).astype(BF16)
            add_side(back, unit_feats, weights, False)


def begin_call(unit_feats, back, protos, last, block):
    width, columns = protos[0].shape
    count = len(protos)
    return call(
        functools.partial(begin_kernel, count, block, last),
        "student_begin",
        shape(back.shape),
        [pltpu.VMEM((width, columns), BF16)] * count + [pltpu.SemaphoreType.DMA((count, last // block))],
        vmem=48 if count > 1 else 16,
        far=range(2, 2 + count),
        flops=4 * unit_feats.shape[0] * count * last * width,
    )(unit_feats, back, *protos)


def other_kernel(count, block, from_column, place, unit_feats, partial, *refs):
    sources, refs = refs[:count], refs[count:]
    outs, refs = refs[: -count - 2], refs[-count - 2 :]
    back, buffers, sems = refs[0], refs[1:-1], refs[-1]
    width = unit_feats.shape[1]
    copies = fetch(sources, buffers, sems, block, from_column)
    back[...] = partial[...]
    add_blocks(copies, buffers, back, unit_feats, block, from_column)
    share = back.shape[0] // len(outs)
    for k, out in enumerate(outs):
        first = pl.multiple_of(jnp.bitwise_xor(place[0], k) * share, share)
        total = back[pl.ds(first, share), :]
        store_code(out, total[:, :width], lane_sums(total[:, width:]))


def other_call(place, unit_feats, back, protos, pieces, from_column, block):
    width, columns = protos[0].shape
    rows = unit_feats.shape[0]
    count = len(protos)
    return call(
        functools.partial(other_kernel, count, block, from_column),
        "student_other",
        [coded(rows // pieces, width)] * pieces,
        [pltpu.VMEM((rows, width + LANES), F32)]
        + [pltpu.VMEM((width, columns), BF16)] * count
        + [pltpu.SemaphoreType.DMA((count, (columns - from_column) // block))],
        scalars=1,
        vmem=48 if count > 1 else 16,
        far=range(3, 3 + count),
        flops=4 * rows * count * columns * width,
    )(place, unit_feats, back, *protos)


def first_kernel(count, block, *refs):
    parts, (weights, plan, sums, unit, partial) = refs[:count], refs[count:]
    columns = weights.shape[1]
    first = 0
    for part in parts:
        images, views, _ = part.shape
        for view in range(views):
            unit[first : first + images, :] = unit_rows(part[:, view, :].astype(F32)).astype(BF16)
            first += images
    for start in range(0, columns, block):
        here = slice(start, start + block)
        column_sums = None
        for first in range(0, unit.shape[0], LANES):
            values = jnp.exp(
                jnp.dot(unit[first : first + LANES, :], weights[:, here], preferred_element_type=F32)
                * (1.0 / teacher_softness)
            )
            plan[first : first + LANES, here] = values
            total = jnp.sum(values, axis=0, keepdims=True)
            column_sums = total if column_sums is None else column_sums + total
        terms = lane_groups(plan[:, here] * (1.0 / column_sums))
        if start == 0:
            partial[...] = terms
        else:
            partial[...] += terms
    store_sums(sums, partial)


def store_sums(sums, partial):
    total = row_vector(partial[...])
    for k in range(sums.shape[0]):
        sums[k] = total


def first_call(parts, weights, copies, block, after=()):
    columns = weights.shape[1]
    rows = sum(part.shape[0] * part.shape[1] for part in parts)
    return call(
        functools.partial(first_kernel, len(parts), block),
        "first_sweep",
        [shape((rows, columns)), shape((copies, 1, rows))],
        [pltpu.VMEM((rows, weights.shape[0]), BF16), pltpu.VMEM((rows, LANES), F32)],
        after=after,
        flops=8 * rows * columns * weights.shape[0],
    )(*parts, weights)


def scale_rows(sum_refs, row_scale):
    scale = 1.0 / read_sums(sum_refs)
    row_scale[...] = jnp.broadcast_to(scale, (LANES, scale.shape[1])).T


def column_scale(plan, row_scale, start):
    weighted = plan[:, start : start + LANES] * row_scale[...]
    return 1.0 / jnp.sum(weighted, axis=0, keepdims=True)


def sweep_kernel(count, share_rows, plan, *refs):
    shares, refs = refs[:count], refs[count:]
    sum_refs, (sums, share, _, row_scale, partial) = refs[:-5] or shares, refs[-5:]
    scale_rows(sum_refs, row_scale)
    for start in range(0, plan.shape[1], LANES):
        terms = plan[:, start : start + LANES] * column_scale(plan, row_scale, start)
        if start == 0:
            partial[...] = terms
        else:
            partial[...] += terms
    store_sums(sums, partial)
    back, totals = decode_sum(shares, share_rows)
    store_code(share, back / totals, totals)


def sweep_call(plan, copies, share_rows, shares, row_sums):
    rows = plan.shape[0]
    return call(
        functools.partial(sweep_kernel, len(shares), share_rows),
        "sweep",
        [shape((copies, 1, rows)), shape(shares[0].shape, I16), shape(plan.shape)],
        [pltpu.VMEM((rows, LANES), F32)] * 2,
        aliases={0: 2},
    )(plan, *shares, *row_sums)


def last_kernel(share, count, block, place, plan, unit_protos, *refs):
    sum_refs, refs = refs[:count], refs[count:]
    outs, (row_scale, scaled, mixed) = refs[:-3], refs[-3:]
    own = scaled.shape[0]
    width, columns = unit_protos.shape
    scale_rows(sum_refs, row_scale)
    for start in range(0, columns, block):
        here = slice(start, start + block)
        total = None
        for group in range(start, start + block, LANES):
            terms = plan[:own, group : group + LANES] * column_scale(plan, row_scale, group)
            total = terms if total is None else total + terms
            scaled[:, group - start : group - start + LANES] = terms.astype(BF16)
        sides = dot_t(scaled[...], unit_protos[:, here])
        if start == 0:
            mixed[:, width:] = total
            mixed[:, :width] = sides
        else:
            mixed[:, width:] += total
            mixed[:, :width] += sides
    for k, out in enumerate(outs):
        first = pl.multiple_of(jnp.bitwise_xor(place[0], k) * share, share)
        out[...] = mixed[pl.ds(first, share), :]


def last_call(place, plan, unit_protos, sums, own, count, block, after=()):
    rows = plan.shape[0]
    width = unit_protos.shape[0]
    share = own // count
    return call(
        functools.partial(last_kernel, share, len(sums), block),
        "last_sweep",
        [shape((share, width + LANES))] * count,
        [
            pltpu.VMEM((rows, LANES), F32),
            pltpu.VMEM((own, block), BF16),
            pltpu.VMEM((own, width + LANES), F32),
        ],
        scalars=1,
        after=after,
    )(place, plan, unit_protos, *sums)


def as_column(row):
    return jnp.broadcast_to(row, (LANES, row.shape[1])).T[:, :1]


def lane_sums(values):
    return jnp.sum(values, axis=1, keepdims=True)


def code_kernel(*refs):
    parts, out = refs[:-1], refs[-1]
    width = parts[0].shape[1] - LANES
    total = tree_sum([part[...] for part in parts])
    store_code(out, total[:, :width], lane_sums(total[:, width:]))


def code_call(parts, after=()):
    rows, columns = parts[0].shape
    out = coded(rows, columns - LANES)
    return call(code_kernel, "code_mixed", out, after=after)(*parts)


def mean_kernel(*refs):
    parts, out = refs[:-1], refs[-1]
    mixed, totals = decode_sum(parts, out.shape[0])
    out[...] = mixed / totals


def mean_call(parts, width, after=()):
    rows = (parts[0].shape[0] - ROW_TILE) * LANES // width
    return call(mean_kernel, "mean_protos", shape((rows, width)), after=after)(*parts)


FIELDS = 4


def prepare_kernel(place, feats, picked, weights, *refs):
    shares, (base, fields, expected, totals) = refs[:-4], refs[-4:]
    rows = expected.shape[0] // len(shares)
    for k, part in enumerate(shares):
        first = pl.multiple_of(jnp.bitwise_xor(place[0], k) * rows, rows)
        values, extra = decode(part, rows)
        expected[pl.ds(first, rows), :] = values
        totals[pl.ds(first, rows), :] = jnp.broadcast_to(extra, (rows, LANES))
    images = feats.shape[1]
    lane = lax.broadcasted_iota(jnp.int32, (images, LANES), 1)
    for crop in range(feats.shape[0]):
        here = slice(crop * images, (crop + 1) * images)
        raw = feats[crop].astype(F32)
        scales = lax.rsqrt(lane_sums(raw * raw) + epsilon)
        factor = as_column(weights[crop : crop + 1, :].astype(F32)) * (scales * (1.0 / student_softness))
        cubic = factor * scales * scales
        mean = expected[here, :]
        base[here, :] = factor * mean - (cubic * lane_sums(raw * mean)) * raw
        logs = jnp.log(totals[here, :])
        view = as_column(picked[crop : crop + 1, :].astype(F32))
        fields[here, :] = jnp.where(
            lane == 0, factor, jnp.where(lane == 1, cubic, jnp.where(lane == 2, scales, logs))
        )
        fields[here, :] = jnp.where(lane == FIELDS, view, fields[here, :])


def prepare_call(place, feats, picked, weights, shares, after=()):
    crops, images, width = feats.shape
    rows = crops * images
    return call(
        prepare_kernel,
        "prepare",
        [shape((rows, width)), shape((rows, LANES))],
        [pltpu.VMEM((rows, width), F32), pltpu.VMEM((rows, LANES), F32)],
        scalars=1,
        after=after,
    )(place, feats, picked, weights, *shares)


def finish_kernel(views, place, feats, base, fields, *refs):
    parts, (gradient, loss, means, ready, sems) = refs[:-5], refs[-5:]
    copies = []
    rows = parts[0].shape[0]
    for k, part in enumerate(parts):
        first = pl.multiple_of(jnp.bitwise_xor(place[0], k) * rows, rows)
        means[pl.ds(first, rows), :] = part[...]
    images = feats.shape[1]
    for crop in range(feats.shape[0]):
        here = slice(crop * images, (crop + 1) * images)
        raw = feats[crop].astype(F32)
        factor, cubic, scales = (fields[here, k : k + 1] for k in range(3))
        view_column = fields[here, FIELDS : FIELDS + 1]
        chosen = means[:images, :]
        for view in range(1, views):
            chosen = jnp.where(view_column == view, means[view * images : (view + 1) * images, :], chosen)
        along = cubic * lane_sums(raw * chosen)
        ready[crop] = base[here, :] - factor * chosen + along * raw
        copies.append(pltpu.make_async_copy(ready.at[crop], gradient.at[crop], sems.at[crop]))
        copies[-1].start()
        unit = (raw * scales).astype(BF16).astype(F32)
        column = fields[here, FIELDS - 1 : FIELDS] - lane_sums(unit * chosen) * (1.0 / student_softness)
        loss[crop : crop + 1, :] = jnp.broadcast_to(column, (images, LANES)).T[:1, :]
    for copy in copies:
        copy.wait()


def finish_call(views, place, feats, base, fields, means):
    crops, images, width = feats.shape
    return call(
        functools.partial(finish_kernel, views),
        "finish",
        [shape((crops, images, width)), shape((crops, images))],
        [
            pltpu.VMEM((views * images, width), F32),
            pltpu.VMEM((crops, images, width), F32),
            pltpu.SemaphoreType.DMA((crops,)),
        ],
        scalars=1,
        far_out=[0],
    )(place, feats, base, fields, *means)


def shards(teacher_feats, student_feats, teacher_protos, student_protos, pairing, row_weight):
    images, views, width = teacher_feats.shape
    crops = student_feats.shape[0]
    image_devices = lax.axis_size("image")
    crop_devices = lax.axis_size("crop")
    proto_devices = lax.axis_size("proto")
    crop_place = lax.axis_index("crop").reshape(1)
    proto_place = lax.axis_index("proto").reshape(1)
    block = 512

    teacher_parts = [teacher_feats] + [swap(teacher_feats, "image", k) for k in range(1, image_devices)]
    feats = student_feats.reshape(crops * images, width)
    protos = [student_protos] + [swap(student_protos, "crop", k) for k in range(1, crop_devices)]

    teacher_rows = image_devices * images * views
    joint = crops * images % (proto_devices * ROW_TILE) == 0 and 3 * teacher_rows == (ROW_TILE - SUMS_AT) * LANES
    pieces, copies = (proto_devices, 1) if joint else (1, crop_devices * proto_devices)
    if not joint:
        proto_place = jnp.zeros((1,), jnp.int32)

    def from_all(shares):
        return [shares[0]] + [swap(shares[k % len(shares)], "proto", k) for k in range(1, proto_devices)]

    def exchange(sums, shares):
        if joint:
            parts = [sums] + [swap(sums, "crop", k) for k in range(1, crop_devices)]
            return from_all(pack_call(parts, shares)), []
        return from_all(shares), [lax.all_to_all(sums, ("crop", "proto"), 0, 0)]

    unit_protos, unit_teacher, unit_feats, back = own_call(
        crop_place, proto_place, feats, student_protos, teacher_protos, block
    )
    half = student_protos.shape[1] // (2 * block) * block
    back = begin_call(unit_feats, back, protos[1:], half, block)
    plan, sums = first_call(teacher_parts, unit_teacher, copies, block, after=[back])
    shares = other_call(proto_place, unit_feats, back, protos[1:], pieces, half, block)
    for _ in range(SWEEPS - 2):
        shares, row_sums = exchange(sums, shares)
        sums, share, plan = sweep_call(plan, copies, crops * images // pieces, shares, row_sums)
        shares = [share]
    if joint:
        shares, row_sums = exchange(sums, shares)
    else:
        row_sums = [lax.all_to_all(sums, ("crop", "proto"), 0, 0)]
    mixed = last_call(
        crop_place, plan, unit_protos, row_sums or shares, views * images, crop_devices, block
    )

    sent = code_call([mixed[0]] + [swap(mixed[k], "crop", k) for k in range(1, crop_devices)])
    base, fields = prepare_call(proto_place, student_feats, pairing, row_weight, shares, after=[sent])
    means = mean_call(from_all([sent]), width, after=[base])
    means = [means] + [swap(means, "crop", k) for k in range(1, crop_devices)]
    return finish_call(views, crop_place, student_feats, base, fields, means)


def solution(mesh):
    in_specs = (
        P("image", None, None),
        P("crop", "image", None),
        P(None, ("crop", "proto")),
        P(None, ("crop", "proto")),
        P("crop", "image"),
        P("crop", "image"),
    )
    out_specs = (P("crop", "image", None), P("crop", "image"))
    return jax.shard_map(shards, mesh=mesh, in_specs=in_specs, out_specs=out_specs, check_vma=False)
```

```python
import functools

import jax
import jax.numpy as jnp
from jax import lax
from jax.experimental import pallas as pl
from jax.experimental.pallas import tpu as pltpu
from jax.sharding import PartitionSpec as P

SWEEPS = 3
LANES = 128
ROW_TILE = 16
LEVELS = 32767.0
PARTS = 32768.0

epsilon = 1e-06
student_softness = 0.1
teacher_softness = 0.04

F32 = jnp.float32
BF16 = jnp.bfloat16
I16 = jnp.int16

IN_VMEM = pl.BlockSpec(memory_space=pltpu.VMEM)
IN_HBM = pl.BlockSpec(memory_space=pltpu.HBM)
IN_SMEM = pl.BlockSpec(memory_space=pltpu.SMEM)


def call(kernel, name, out_shape, scratch=(), scalars=0, vmem=16, after=(), flops=10**9, aliases=None, far=()):
    def run(*operands):
        count = len(operands)

        def body(*refs):
            kernel(*refs[:count], *refs[count + len(after) :])

        return pl.pallas_call(
            body,
            in_specs=[IN_SMEM] * scalars
            + [IN_HBM if i in far else IN_VMEM for i in range(scalars, count)]
            + [pl.BlockSpec(memory_space=pl.ANY)] * len(after),
            out_specs=jax.tree.map(lambda _: IN_VMEM, out_shape),
            out_shape=out_shape,
            scratch_shapes=list(scratch),
            compiler_params=pltpu.CompilerParams(vmem_limit_bytes=vmem * 1024 * 1024),
            cost_estimate=pl.CostEstimate(flops=flops, bytes_accessed=0, transcendentals=0),
            input_output_aliases=aliases or {},
            name=name,
        )(*operands, *after)

    return run


def shape(dims, dtype=F32):
    return jax.ShapeDtypeStruct(dims, dtype)


def unit_rows(raw_rows):
    return raw_rows * lax.rsqrt(jnp.sum(raw_rows * raw_rows, axis=-1, keepdims=True) + epsilon)


def unit_columns(entries):
    return entries * lax.rsqrt(jnp.sum(entries * entries, axis=0, keepdims=True) + epsilon)


def lane_groups(values):
    total = values[:, :LANES]
    for start in range(LANES, values.shape[1], LANES):
        total = total + values[:, start : start + LANES]
    return total


def dot_t(a, b):
    return lax.dot_general(a, b, (((1,), (1,)), ((), ())), preferred_element_type=F32)


def row_vector(partial):
    return jnp.sum(partial.T, axis=0, keepdims=True)


def tree_sum(terms):
    while len(terms) > 1:
        terms = [terms[i] + terms[i + 1] for i in range(0, len(terms), 2)]
    return terms[0]


def split_positive(values):
    power = jnp.floor(jnp.log2(jnp.maximum(values, 1e-30))) + 1.0
    scaled = values * jnp.exp2(-power) * PARTS
    high = jnp.minimum(jnp.floor(scaled), LEVELS)
    low = jnp.minimum(jnp.floor((scaled - high) * PARTS), LEVELS)
    return power, high, low


def join_positive(power, high, low):
    return (high + low * (1.0 / PARTS)) * (1.0 / PARTS) * jnp.exp2(power)


def to_i16(values):
    return values.astype(jnp.int32).astype(I16)


def to_f32(values):
    return values.astype(jnp.int32).astype(F32)


def coded(rows, width):
    return jax.ShapeDtypeStruct((rows * width // LANES + ROW_TILE, LANES), I16)


def store_code(out, values, extra):
    rows, width = values.shape
    largest = jnp.maximum(jnp.max(jnp.abs(values), axis=1, keepdims=True), 1e-30)
    power = jnp.floor(jnp.log2(largest)) + 1.0
    whole = jnp.floor(values * (jnp.exp2(-power) * LEVELS) + 0.5)
    whole = to_i16(jnp.clip(whole, -LEVELS, LEVELS))
    for k in range(width // LANES):
        out[k * rows : (k + 1) * rows, :] = whole[:, k * LANES : (k + 1) * LANES]
    extra_power, high, low = split_positive(extra)
    lane = lax.broadcasted_iota(jnp.int32, (rows, LANES), 1)
    tail = jnp.where(lane == 0, power, jnp.where(lane == 1, extra_power, jnp.where(lane == 2, high, low)))
    if rows < LANES:
        tail = jnp.concatenate([tail, jnp.zeros((LANES - rows, LANES), F32)], axis=0)
    out[out.shape[0] - ROW_TILE :, :] = to_i16(tail.T[:ROW_TILE, :])


def decode(ref, rows):
    count = (ref.shape[0] - ROW_TILE) // rows
    block = to_f32(ref[count * rows :, :])
    tail = jnp.concatenate([block, jnp.zeros((LANES - ROW_TILE, LANES), F32)], axis=0).T[:rows, :]
    values = jnp.concatenate([to_f32(ref[k * rows : (k + 1) * rows, :]) for k in range(count)], axis=1)
    values = values * (jnp.exp2(tail[:, 0:1]) * (1.0 / LEVELS))
    return values, join_positive(tail[:, 1:2], tail[:, 2:3], tail[:, 3:4])


def decode_sum(refs, rows):
    pairs = [decode(ref, rows) for ref in refs]
    return tree_sum([p[0] for p in pairs]), tree_sum([p[1] for p in pairs])


SUMS_AT = 4


def pack_kernel(count, *refs):
    parts, refs = refs[:count], refs[count:]
    shares, outs = refs[: len(refs) // 2], refs[len(refs) // 2 :]
    terms = split_positive(tree_sum([part[0] for part in parts]))
    groups = terms[0].shape[1] // LANES
    for share, out in zip(shares, outs):
        last = share.shape[0] - ROW_TILE
        out[:last, :] = share[:last, :]
        at = lax.broadcasted_iota(jnp.int32, (ROW_TILE, LANES), 0)
        under = to_f32(share[last:, :])
        for k, row in enumerate(terms):
            for j in range(groups):
                piece = row[:, j * LANES : (j + 1) * LANES]
                under = jnp.where(at == SUMS_AT + k * groups + j, piece, under)
        out[last:, :] = to_i16(under)


def pack_call(parts, shares):
    return call(
        functools.partial(pack_kernel, len(parts)),
        "pack_sums",
        [shape(share.shape, I16) for share in shares],
    )(*parts, *shares)


def read_sums(refs):
    if refs[0].dtype == I16:
        terms = []
        groups = (ROW_TILE - SUMS_AT) // 3
        for ref in refs:
            under = to_f32(ref[ref.shape[0] - ROW_TILE :, :])
            rows = [
                jnp.concatenate([under[at + j : at + j + 1, :] for j in range(groups)], axis=1)
                for at in range(SUMS_AT, SUMS_AT + 3 * groups, groups)
            ]
            terms.append(join_positive(*rows))
        return tree_sum(terms)
    total = refs[0][0]
    for k in range(1, refs[0].shape[0]):
        total = total + refs[0][k]
    return total


def swap(values, axis, distance):
    count = lax.axis_size(axis)
    return lax.ppermute(values, axis, [(i, i ^ distance) for i in range(count)])


def fetch(sources, buffers, sems, block, first=0, last=None):
    last = buffers[0].shape[1] if last is None else last
    copies = []
    for j, start in enumerate(range(first, last, block)):
        here = pl.ds(start, block)
        copies.append(
            [
                pltpu.make_async_copy(source.at[:, here], buffer.at[:, here], sems.at[i, j])
                for i, (source, buffer) in enumerate(zip(sources, buffers))
            ]
        )
    for group in copies:
        for copy in group:
            copy.start()
    return copies


def add_side(back, unit_feats, weights, fresh):
    width = weights.shape[0]
    logits = jnp.dot(unit_feats[...], weights, preferred_element_type=F32)
    terms = jnp.exp(logits * (1.0 / student_softness))
    sums = lane_groups(terms)
    sides = dot_t(terms.astype(BF16), weights)
    if fresh:
        back[:, width:] = sums
        back[:, :width] = sides
    else:
        back[:, width:] += sums
        back[:, :width] += sides


def own_kernel(block, crop_place, proto_place, feats, protos, teacher_protos, unit_protos, unit_teacher, unit_feats, back, *refs):
    raw, buffers, raw_sem, sems = refs[0], refs[1:3], refs[3], refs[4]
    raw_copy = pltpu.make_async_copy(feats, raw, raw_sem)
    raw_copy.start()
    copies = fetch([protos, teacher_protos], buffers, sems, block)
    raw_copy.wait()
    unit_feats[...] = unit_rows(raw[...].astype(F32)).astype(BF16)
    for j, group in enumerate(copies):
        here = slice(j * block, (j + 1) * block)
        group[0].wait()
        weights = unit_columns(buffers[0][:, here].astype(F32)).astype(BF16)
        unit_protos[:, here] = weights
        add_side(back, unit_feats, weights, j == 0)
        group[1].wait()
        unit_teacher[:, here] = unit_columns(buffers[1][:, here].astype(F32)).astype(BF16)


def own_call(crop_place, proto_place, feats, protos, teacher_protos, block):
    width, columns = protos.shape
    rows = feats.shape[0]
    return call(
        functools.partial(own_kernel, block),
        "student_own",
        [shape((width, columns), BF16)] * 2 + [shape((rows, width), BF16), shape((rows, width + LANES))],
        [pltpu.VMEM((rows, width), BF16)]
        + [pltpu.VMEM((width, columns), BF16)] * 2
        + [pltpu.SemaphoreType.DMA, pltpu.SemaphoreType.DMA((2, columns // block))],
        scalars=2,
        vmem=47,
        far=[2, 3, 4],
        flops=4 * rows * columns * width,
    )(crop_place, proto_place, feats, protos, teacher_protos)


def begin_kernel(count, block, last, unit_feats, partial, *refs):
    sources, (back, *buffers, sems) = refs[:count], refs[count:]
    copies = fetch(sources, buffers, sems, block, 0, last)
    back[...] = partial[...]
    add_blocks(copies, buffers, back, unit_feats, block, 0)


def add_blocks(copies, buffers, back, unit_feats, block, first):
    for j, group in enumerate(copies):
        here = slice(first + j * block, first + (j + 1) * block)
        for copy, buffer in zip(group, buffers):
            copy.wait()
            weights = unit_columns(buffer[:, here].astype(F32)).astype(BF16)
            add_side(back, unit_feats, weights, False)


def begin_call(unit_feats, back, protos, last, block):
    width, columns = protos[0].shape
    count = len(protos)
    return call(
        functools.partial(begin_kernel, count, block, last),
        "student_begin",
        shape(back.shape),
        [pltpu.VMEM((width, columns), BF16)] * count + [pltpu.SemaphoreType.DMA((count, last // block))],
        vmem=48 if count > 1 else 16,
        far=range(2, 2 + count),
        flops=4 * unit_feats.shape[0] * count * last * width,
    )(unit_feats, back, *protos)


def other_kernel(count, block, from_column, place, unit_feats, partial, *refs):
    sources, refs = refs[:count], refs[count:]
    outs, refs = refs[: -count - 2], refs[-count - 2 :]
    back, buffers, sems = refs[0], refs[1:-1], refs[-1]
    width = unit_feats.shape[1]
    copies = fetch(sources, buffers, sems, block, from_column)
    back[...] = partial[...]
    add_blocks(copies, buffers, back, unit_feats, block, from_column)
    share = back.shape[0] // len(outs)
    for k, out in enumerate(outs):
        first = pl.multiple_of(jnp.bitwise_xor(place[0], k) * share, share)
        total = back[pl.ds(first, share), :]
        store_code(out, total[:, :width], lane_sums(total[:, width:]))


def other_call(place, unit_feats, back, protos, pieces, from_column, block):
    width, columns = protos[0].shape
    rows = unit_feats.shape[0]
    count = len(protos)
    return call(
        functools.partial(other_kernel, count, block, from_column),
        "student_other",
        [coded(rows // pieces, width)] * pieces,
        [pltpu.VMEM((rows, width + LANES), F32)]
        + [pltpu.VMEM((width, columns), BF16)] * count
        + [pltpu.SemaphoreType.DMA((count, (columns - from_column) // block))],
        scalars=1,
        vmem=48 if count > 1 else 16,
        far=range(3, 3 + count),
        flops=4 * rows * count * columns * width,
    )(place, unit_feats, back, *protos)


def first_kernel(count, block, *refs):
    parts, (weights, plan, sums, unit, partial) = refs[:count], refs[count:]
    columns = weights.shape[1]
    first = 0
    for part in parts:
        images, views, _ = part.shape
        for view in range(views):
            unit[first : first + images, :] = unit_rows(part[:, view, :].astype(F32)).astype(BF16)
            first += images
    for start in range(0, columns, block):
        here = slice(start, start + block)
        column_sums = None
        for first in range(0, unit.shape[0], LANES):
            values = jnp.exp(
                jnp.dot(unit[first : first + LANES, :], weights[:, here], preferred_element_type=F32)
                * (1.0 / teacher_softness)
            )
            plan[first : first + LANES, here] = values
            total = jnp.sum(values, axis=0, keepdims=True)
            column_sums = total if column_sums is None else column_sums + total
        terms = lane_groups(plan[:, here] * (1.0 / column_sums))
        if start == 0:
            partial[...] = terms
        else:
            partial[...] += terms
    store_sums(sums, partial)


def store_sums(sums, partial):
    total = row_vector(partial[...])
    for k in range(sums.shape[0]):
        sums[k] = total


def first_call(parts, weights, copies, block, after=()):
    columns = weights.shape[1]
    rows = sum(part.shape[0] * part.shape[1] for part in parts)
    return call(
        functools.partial(first_kernel, len(parts), block),
        "first_sweep",
        [shape((rows, columns)), shape((copies, 1, rows))],
        [pltpu.VMEM((rows, weights.shape[0]), BF16), pltpu.VMEM((rows, LANES), F32)],
        after=after,
        flops=8 * rows * columns * weights.shape[0],
    )(*parts, weights)


def scale_rows(sum_refs, row_scale):
    scale = 1.0 / read_sums(sum_refs)
    row_scale[...] = jnp.broadcast_to(scale, (LANES, scale.shape[1])).T


def column_scale(plan, row_scale, start):
    weighted = plan[:, start : start + LANES] * row_scale[...]
    return 1.0 / jnp.sum(weighted, axis=0, keepdims=True)


def sweep_kernel(plan, *refs):
    sum_refs, (sums, _, row_scale, partial) = refs[:-4], refs[-4:]
    scale_rows(sum_refs, row_scale)
    for start in range(0, plan.shape[1], LANES):
        terms = plan[:, start : start + LANES] * column_scale(plan, row_scale, start)
        if start == 0:
            partial[...] = terms
        else:
            partial[...] += terms
    store_sums(sums, partial)


def sweep_call(plan, copies, row_sums):
    rows = plan.shape[0]
    return call(
        sweep_kernel,
        "sweep",
        [shape((copies, 1, rows)), shape(plan.shape)],
        [pltpu.VMEM((rows, LANES), F32)] * 2,
        aliases={0: 1},
    )(plan, *row_sums)


def total_kernel(rows, *refs):
    shares, share = refs[:-1], refs[-1]
    back, totals = decode_sum(shares, rows)
    store_code(share, back / totals, totals)


def total_call(shares, rows, after):
    out = shape(shares[0].shape, I16)
    return call(functools.partial(total_kernel, rows), "student_totals", out, after=after)(*shares)


def last_kernel(share, count, block, place, plan, unit_protos, *refs):
    sum_refs, refs = refs[:count], refs[count:]
    outs, (row_scale, scaled, mixed) = refs[:-3], refs[-3:]
    own = scaled.shape[0]
    width, columns = unit_protos.shape
    scale_rows(sum_refs, row_scale)
    for start in range(0, columns, block):
        here = slice(start, start + block)
        total = None
        for group in range(start, start + block, LANES):
            terms = plan[:own, group : group + LANES] * column_scale(plan, row_scale, group)
            total = terms if total is None else total + terms
            scaled[:, group - start : group - start + LANES] = terms.astype(BF16)
        sides = dot_t(scaled[...], unit_protos[:, here])
        if start == 0:
            mixed[:, width:] = total
            mixed[:, :width] = sides
        else:
            mixed[:, width:] += total
            mixed[:, :width] += sides
    for k, out in enumerate(outs):
        first = pl.multiple_of(jnp.bitwise_xor(place[0], k) * share, share)
        out[...] = mixed[pl.ds(first, share), :]


def last_call(place, plan, unit_protos, sums, own, count, block, after=()):
    rows = plan.shape[0]
    width = unit_protos.shape[0]
    share = own // count
    return call(
        functools.partial(last_kernel, share, len(sums), block),
        "last_sweep",
        [shape((share, width + LANES))] * count,
        [
            pltpu.VMEM((rows, LANES), F32),
            pltpu.VMEM((own, block), BF16),
            pltpu.VMEM((own, width + LANES), F32),
        ],
        scalars=1,
        after=after,
    )(place, plan, unit_protos, *sums)


def as_column(row):
    return jnp.broadcast_to(row, (LANES, row.shape[1])).T[:, :1]


def lane_sums(values):
    return jnp.sum(values, axis=1, keepdims=True)


def code_kernel(*refs):
    parts, out = refs[:-1], refs[-1]
    width = parts[0].shape[1] - LANES
    total = tree_sum([part[...] for part in parts])
    store_code(out, total[:, :width], lane_sums(total[:, width:]))


def code_call(parts, after=()):
    rows, columns = parts[0].shape
    out = coded(rows, columns - LANES)
    return call(code_kernel, "code_mixed", out, after=after)(*parts)


def mean_kernel(*refs):
    parts, out = refs[:-1], refs[-1]
    mixed, totals = decode_sum(parts, out.shape[0])
    out[...] = mixed / totals


def mean_call(parts, width, after=()):
    rows = (parts[0].shape[0] - ROW_TILE) * LANES // width
    return call(mean_kernel, "mean_protos", shape((rows, width)), after=after)(*parts)


FIELDS = 4


def prepare_kernel(place, feats, picked, weights, *refs):
    shares, (base, fields, expected, totals) = refs[:-4], refs[-4:]
    rows = expected.shape[0] // len(shares)
    for k, part in enumerate(shares):
        first = pl.multiple_of(jnp.bitwise_xor(place[0], k) * rows, rows)
        values, extra = decode(part, rows)
        expected[pl.ds(first, rows), :] = values
        totals[pl.ds(first, rows), :] = jnp.broadcast_to(extra, (rows, LANES))
    images = feats.shape[1]
    lane = lax.broadcasted_iota(jnp.int32, (images, LANES), 1)
    for crop in range(feats.shape[0]):
        here = slice(crop * images, (crop + 1) * images)
        raw = feats[crop].astype(F32)
        scales = lax.rsqrt(lane_sums(raw * raw) + epsilon)
        factor = as_column(weights[crop : crop + 1, :].astype(F32)) * (scales * (1.0 / student_softness))
        cubic = factor * scales * scales
        mean = expected[here, :]
        base[here, :] = factor * mean - (cubic * lane_sums(raw * mean)) * raw
        logs = jnp.log(totals[here, :])
        view = as_column(picked[crop : crop + 1, :].astype(F32))
        fields[here, :] = jnp.where(
            lane == 0, factor, jnp.where(lane == 1, cubic, jnp.where(lane == 2, scales, logs))
        )
        fields[here, :] = jnp.where(lane == FIELDS, view, fields[here, :])


def prepare_call(place, feats, picked, weights, shares, after=()):
    crops, images, width = feats.shape
    rows = crops * images
    return call(
        prepare_kernel,
        "prepare",
        [shape((rows, width)), shape((rows, LANES))],
        [pltpu.VMEM((rows, width), F32), pltpu.VMEM((rows, LANES), F32)],
        scalars=1,
        after=after,
    )(place, feats, picked, weights, *shares)


def finish_kernel(views, place, feats, base, fields, *refs):
    parts, (gradient, loss, means) = refs[:-3], refs[-3:]
    rows = parts[0].shape[0]
    for k, part in enumerate(parts):
        first = pl.multiple_of(jnp.bitwise_xor(place[0], k) * rows, rows)
        means[pl.ds(first, rows), :] = part[...]
    images = feats.shape[1]
    for crop in range(feats.shape[0]):
        here = slice(crop * images, (crop + 1) * images)
        raw = feats[crop].astype(F32)
        factor, cubic, scales = (fields[here, k : k + 1] for k in range(3))
        view_column = fields[here, FIELDS : FIELDS + 1]
        chosen = means[:images, :]
        for view in range(1, views):
            chosen = jnp.where(view_column == view, means[view * images : (view + 1) * images, :], chosen)
        along = cubic * lane_sums(raw * chosen)
        gradient[crop] = base[here, :] - factor * chosen + along * raw
        unit = (raw * scales).astype(BF16).astype(F32)
        column = fields[here, FIELDS - 1 : FIELDS] - lane_sums(unit * chosen) * (1.0 / student_softness)
        loss[crop : crop + 1, :] = jnp.broadcast_to(column, (images, LANES)).T[:1, :]


def finish_call(views, place, feats, base, fields, means):
    crops, images, width = feats.shape
    return call(
        functools.partial(finish_kernel, views),
        "finish",
        [shape((crops, images, width)), shape((crops, images))],
        [pltpu.VMEM((views * images, width), F32)],
        scalars=1,
    )(place, feats, base, fields, *means)


def shards(teacher_feats, student_feats, teacher_protos, student_protos, pairing, row_weight):
    images, views, width = teacher_feats.shape
    crops = student_feats.shape[0]
    image_devices = lax.axis_size("image")
    crop_devices = lax.axis_size("crop")
    proto_devices = lax.axis_size("proto")
    crop_place = lax.axis_index("crop").reshape(1)
    proto_place = lax.axis_index("proto").reshape(1)
    block = 512

    teacher_parts = [teacher_feats] + [swap(teacher_feats, "image", k) for k in range(1, image_devices)]
    feats = student_feats.reshape(crops * images, width)
    protos = [student_protos] + [swap(student_protos, "crop", k) for k in range(1, crop_devices)]

    teacher_rows = image_devices * images * views
    joint = crops * images % (proto_devices * ROW_TILE) == 0 and 3 * teacher_rows == (ROW_TILE - SUMS_AT) * LANES
    pieces, copies = (proto_devices, 1) if joint else (1, crop_devices * proto_devices)
    if not joint:
        proto_place = jnp.zeros((1,), jnp.int32)

    def from_all(shares):
        return [shares[0]] + [swap(shares[k % len(shares)], "proto", k) for k in range(1, proto_devices)]

    def exchange(sums, shares):
        if joint:
            parts = [sums] + [swap(sums, "crop", k) for k in range(1, crop_devices)]
            return from_all(pack_call(parts, shares)), []
        return from_all(shares), [lax.all_to_all(sums, ("crop", "proto"), 0, 0)]

    unit_protos, unit_teacher, unit_feats, back = own_call(
        crop_place, proto_place, feats, student_protos, teacher_protos, block
    )
    half = student_protos.shape[1] // (2 * block) * block
    back = begin_call(unit_feats, back, protos[1:], half, block)
    plan, sums = first_call(teacher_parts, unit_teacher, copies, block, after=[back])
    shares = other_call(proto_place, unit_feats, back, protos[1:], pieces, half, block)
    for _ in range(SWEEPS - 2):
        shares, row_sums = exchange(sums, shares)
        sums, plan = sweep_call(plan, copies, row_sums or shares)
        shares = [total_call(shares, crops * images // pieces, [sums])]
    if joint:
        shares, row_sums = exchange(sums, shares)
    else:
        row_sums = [lax.all_to_all(sums, ("crop", "proto"), 0, 0)]
    mixed = last_call(
        crop_place, plan, unit_protos, row_sums or shares, views * images, crop_devices, block
    )

    sent = code_call([mixed[0]] + [swap(mixed[k], "crop", k) for k in range(1, crop_devices)])
    base, fields = prepare_call(proto_place, student_feats, pairing, row_weight, shares, after=[sent])
    means = mean_call(from_all([sent]), width, after=[base])
    means = [means] + [swap(means, "crop", k) for k in range(1, crop_devices)]
    return finish_call(views, crop_place, student_feats, base, fields, means)


def solution(mesh):
    in_specs = (
        P("image", None, None),
        P("crop", "image", None),
        P(None, ("crop", "proto")),
        P(None, ("crop", "proto")),
        P("crop", "image"),
        P("crop", "image"),
    )
    out_specs = (P("crop", "image", None), P("crop", "image"))
    return jax.shard_map(shards, mesh=mesh, in_specs=in_specs, out_specs=out_specs, check_vma=False)
```

```python
import functools

import jax
import jax.numpy as jnp
from jax import lax
from jax.experimental import pallas as pl
from jax.experimental.pallas import tpu as pltpu
from jax.sharding import PartitionSpec as P

SWEEPS = 3
LANES = 128
ROW_TILE = 16
LEVELS = 32767.0
PARTS = 32768.0

epsilon = 1e-06
student_softness = 0.1
teacher_softness = 0.04

F32 = jnp.float32
BF16 = jnp.bfloat16
I16 = jnp.int16

IN_VMEM = pl.BlockSpec(memory_space=pltpu.VMEM)
IN_HBM = pl.BlockSpec(memory_space=pltpu.HBM)
IN_SMEM = pl.BlockSpec(memory_space=pltpu.SMEM)


def call(kernel, name, out_shape, scratch=(), scalars=0, vmem=16, after=(), flops=10**9, aliases=None, far=()):
    def run(*operands):
        count = len(operands)

        def body(*refs):
            kernel(*refs[:count], *refs[count + len(after) :])

        return pl.pallas_call(
            body,
            in_specs=[IN_SMEM] * scalars
            + [IN_HBM if i in far else IN_VMEM for i in range(scalars, count)]
            + [pl.BlockSpec(memory_space=pl.ANY)] * len(after),
            out_specs=jax.tree.map(lambda _: IN_VMEM, out_shape),
            out_shape=out_shape,
            scratch_shapes=list(scratch),
            compiler_params=pltpu.CompilerParams(vmem_limit_bytes=vmem * 1024 * 1024),
            cost_estimate=pl.CostEstimate(flops=flops, bytes_accessed=0, transcendentals=0),
            input_output_aliases=aliases or {},
            name=name,
        )(*operands, *after)

    return run


def shape(dims, dtype=F32):
    return jax.ShapeDtypeStruct(dims, dtype)


def unit_rows(raw_rows):
    return raw_rows * lax.rsqrt(jnp.sum(raw_rows * raw_rows, axis=-1, keepdims=True) + epsilon)


def unit_columns(entries):
    return entries * lax.rsqrt(jnp.sum(entries * entries, axis=0, keepdims=True) + epsilon)


def lane_groups(values):
    total = values[:, :LANES]
    for start in range(LANES, values.shape[1], LANES):
        total = total + values[:, start : start + LANES]
    return total


def dot_t(a, b):
    return lax.dot_general(a, b, (((1,), (1,)), ((), ())), preferred_element_type=F32)


def row_vector(partial):
    return jnp.sum(partial.T, axis=0, keepdims=True)


def tree_sum(terms):
    while len(terms) > 1:
        terms = [terms[i] + terms[i + 1] for i in range(0, len(terms), 2)]
    return terms[0]


def split_positive(values):
    power = jnp.floor(jnp.log2(jnp.maximum(values, 1e-30))) + 1.0
    scaled = values * jnp.exp2(-power) * PARTS
    high = jnp.minimum(jnp.floor(scaled), LEVELS)
    low = jnp.minimum(jnp.floor((scaled - high) * PARTS), LEVELS)
    return power, high, low


def join_positive(power, high, low):
    return (high + low * (1.0 / PARTS)) * (1.0 / PARTS) * jnp.exp2(power)


def to_i16(values):
    return values.astype(jnp.int32).astype(I16)


def to_f32(values):
    return values.astype(jnp.int32).astype(F32)


def coded(rows, width):
    return jax.ShapeDtypeStruct((rows * width // LANES + ROW_TILE, LANES), I16)


def store_code(out, values, extra):
    rows, width = values.shape
    largest = jnp.maximum(jnp.max(jnp.abs(values), axis=1, keepdims=True), 1e-30)
    power = jnp.floor(jnp.log2(largest)) + 1.0
    whole = jnp.floor(values * (jnp.exp2(-power) * LEVELS) + 0.5)
    whole = to_i16(jnp.clip(whole, -LEVELS, LEVELS))
    for k in range(width // LANES):
        out[k * rows : (k + 1) * rows, :] = whole[:, k * LANES : (k + 1) * LANES]
    extra_power, high, low = split_positive(extra)
    lane = lax.broadcasted_iota(jnp.int32, (rows, LANES), 1)
    tail = jnp.where(lane == 0, power, jnp.where(lane == 1, extra_power, jnp.where(lane == 2, high, low)))
    if rows < LANES:
        tail = jnp.concatenate([tail, jnp.zeros((LANES - rows, LANES), F32)], axis=0)
    out[out.shape[0] - ROW_TILE :, :] = to_i16(tail.T[:ROW_TILE, :])


def decode(ref, rows):
    count = (ref.shape[0] - ROW_TILE) // rows
    block = to_f32(ref[count * rows :, :])
    tail = jnp.concatenate([block, jnp.zeros((LANES - ROW_TILE, LANES), F32)], axis=0).T[:rows, :]
    values = jnp.concatenate([to_f32(ref[k * rows : (k + 1) * rows, :]) for k in range(count)], axis=1)
    values = values * (jnp.exp2(tail[:, 0:1]) * (1.0 / LEVELS))
    return values, join_positive(tail[:, 1:2], tail[:, 2:3], tail[:, 3:4])


def decode_sum(refs, rows):
    pairs = [decode(ref, rows) for ref in refs]
    return tree_sum([p[0] for p in pairs]), tree_sum([p[1] for p in pairs])


SUMS_AT = 4


def pack_kernel(count, *refs):
    parts, refs = refs[:count], refs[count:]
    shares, outs = refs[: len(refs) // 2], refs[len(refs) // 2 :]
    terms = split_positive(tree_sum([part[0] for part in parts]))
    groups = terms[0].shape[1] // LANES
    for share, out in zip(shares, outs):
        last = share.shape[0] - ROW_TILE
        out[:last, :] = share[:last, :]
        at = lax.broadcasted_iota(jnp.int32, (ROW_TILE, LANES), 0)
        under = to_f32(share[last:, :])
        for k, row in enumerate(terms):
            for j in range(groups):
                piece = row[:, j * LANES : (j + 1) * LANES]
                under = jnp.where(at == SUMS_AT + k * groups + j, piece, under)
        out[last:, :] = to_i16(under)


def pack_call(parts, shares):
    return call(
        functools.partial(pack_kernel, len(parts)),
        "pack_sums",
        [shape(share.shape, I16) for share in shares],
    )(*parts, *shares)


def read_sums(refs):
    if refs[0].dtype == I16:
        terms = []
        groups = (ROW_TILE - SUMS_AT) // 3
        for ref in refs:
            under = to_f32(ref[ref.shape[0] - ROW_TILE :, :])
            rows = [
                jnp.concatenate([under[at + j : at + j + 1, :] for j in range(groups)], axis=1)
                for at in range(SUMS_AT, SUMS_AT + 3 * groups, groups)
            ]
            terms.append(join_positive(*rows))
        return tree_sum(terms)
    total = refs[0][0]
    for k in range(1, refs[0].shape[0]):
        total = total + refs[0][k]
    return total


def swap(values, axis, distance):
    count = lax.axis_size(axis)
    return lax.ppermute(values, axis, [(i, i ^ distance) for i in range(count)])


def fetch(sources, buffers, sems, block, first=0, last=None):
    last = buffers[0].shape[1] if last is None else last
    copies = []
    for j, start in enumerate(range(first, last, block)):
        here = pl.ds(start, block)
        copies.append(
            [
                pltpu.make_async_copy(source.at[:, here], buffer.at[:, here], sems.at[i, j])
                for i, (source, buffer) in enumerate(zip(sources, buffers))
            ]
        )
    for group in copies:
        for copy in group:
            copy.start()
    return copies


def add_side(back, unit_feats, weights, fresh):
    width = weights.shape[0]
    logits = jnp.dot(unit_feats[...], weights, preferred_element_type=F32)
    terms = jnp.exp(logits * (1.0 / student_softness))
    sums = lane_groups(terms)
    sides = dot_t(terms.astype(BF16), weights)
    if fresh:
        back[:, width:] = sums
        back[:, :width] = sides
    else:
        back[:, width:] += sums
        back[:, :width] += sides


def own_kernel(block, crop_place, proto_place, feats, protos, teacher_protos, unit_protos, unit_teacher, unit_feats, back, *refs):
    raw, buffers, raw_sem, sems = refs[0], refs[1:3], refs[3], refs[4]
    raw_copy = pltpu.make_async_copy(feats, raw, raw_sem)
    raw_copy.start()
    copies = fetch([protos, teacher_protos], buffers, sems, block)
    raw_copy.wait()
    unit_feats[...] = unit_rows(raw[...].astype(F32)).astype(BF16)
    for j, group in enumerate(copies):
        here = slice(j * block, (j + 1) * block)
        group[0].wait()
        weights = unit_columns(buffers[0][:, here].astype(F32)).astype(BF16)
        unit_protos[:, here] = weights
        add_side(back, unit_feats, weights, j == 0)
        group[1].wait()
        unit_teacher[:, here] = unit_columns(buffers[1][:, here].astype(F32)).astype(BF16)


def own_call(crop_place, proto_place, feats, protos, teacher_protos, block):
    width, columns = protos.shape
    rows = feats.shape[0]
    return call(
        functools.partial(own_kernel, block),
        "student_own",
        [shape((width, columns), BF16)] * 2 + [shape((rows, width), BF16), shape((rows, width + LANES))],
        [pltpu.VMEM((rows, width), BF16)]
        + [pltpu.VMEM((width, columns), BF16)] * 2
        + [pltpu.SemaphoreType.DMA, pltpu.SemaphoreType.DMA((2, columns // block))],
        scalars=2,
        vmem=47,
        far=[2, 3, 4],
        flops=4 * rows * columns * width,
    )(crop_place, proto_place, feats, protos, teacher_protos)


def begin_kernel(count, block, last, unit_feats, partial, *refs):
    sources, (back, *buffers, sems) = refs[:count], refs[count:]
    copies = fetch(sources, buffers, sems, block, 0, last)
    back[...] = partial[...]
    add_blocks(copies, buffers, back, unit_feats, block, 0)


def add_blocks(copies, buffers, back, unit_feats, block, first):
    for j, group in enumerate(copies):
        here = slice(first + j * block, first + (j + 1) * block)
        for copy, buffer in zip(group, buffers):
            copy.wait()
            weights = unit_columns(buffer[:, here].astype(F32)).astype(BF16)
            add_side(back, unit_feats, weights, False)


def begin_call(unit_feats, back, protos, last, block):
    width, columns = protos[0].shape
    count = len(protos)
    return call(
        functools.partial(begin_kernel, count, block, last),
        "student_begin",
        shape(back.shape),
        [pltpu.VMEM((width, columns), BF16)] * count + [pltpu.SemaphoreType.DMA((count, last // block))],
        vmem=48 if count > 1 else 16,
        far=range(2, 2 + count),
        flops=4 * unit_feats.shape[0] * count * last * width,
    )(unit_feats, back, *protos)


def other_kernel(count, block, from_column, place, unit_feats, partial, *refs):
    sources, refs = refs[:count], refs[count:]
    outs, refs = refs[: -count - 2], refs[-count - 2 :]
    back, buffers, sems = refs[0], refs[1:-1], refs[-1]
    width = unit_feats.shape[1]
    copies = fetch(sources, buffers, sems, block, from_column)
    back[...] = partial[...]
    add_blocks(copies, buffers, back, unit_feats, block, from_column)
    share = back.shape[0] // len(outs)
    for k, out in enumerate(outs):
        first = pl.multiple_of(jnp.bitwise_xor(place[0], k) * share, share)
        total = back[pl.ds(first, share), :]
        store_code(out, total[:, :width], lane_sums(total[:, width:]))


def other_call(place, unit_feats, back, protos, pieces, from_column, block):
    width, columns = protos[0].shape
    rows = unit_feats.shape[0]
    count = len(protos)
    return call(
        functools.partial(other_kernel, count, block, from_column),
        "student_other",
        [coded(rows // pieces, width)] * pieces,
        [pltpu.VMEM((rows, width + LANES), F32)]
        + [pltpu.VMEM((width, columns), BF16)] * count
        + [pltpu.SemaphoreType.DMA((count, (columns - from_column) // block))],
        scalars=1,
        vmem=48 if count > 1 else 16,
        far=range(3, 3 + count),
        flops=4 * rows * count * columns * width,
    )(place, unit_feats, back, *protos)


def first_kernel(count, block, *refs):
    parts, (weights, plan, sums, unit, partial) = refs[:count], refs[count:]
    columns = weights.shape[1]
    first = 0
    for part in parts:
        images, views, _ = part.shape
        for view in range(views):
            unit[first : first + images, :] = unit_rows(part[:, view, :].astype(F32)).astype(BF16)
            first += images
    for start in range(0, columns, block):
        here = slice(start, start + block)
        column_sums = None
        for first in range(0, unit.shape[0], LANES):
            values = jnp.exp(
                jnp.dot(unit[first : first + LANES, :], weights[:, here], preferred_element_type=F32)
                * (1.0 / teacher_softness)
            )
            plan[first : first + LANES, here] = values
            total = jnp.sum(values, axis=0, keepdims=True)
            column_sums = total if column_sums is None else column_sums + total
        terms = lane_groups(plan[:, here] * (1.0 / column_sums))
        if start == 0:
            partial[...] = terms
        else:
            partial[...] += terms
    store_sums(sums, partial)


def store_sums(sums, partial):
    total = row_vector(partial[...])
    for k in range(sums.shape[0]):
        sums[k] = total


def first_call(parts, weights, copies, block, after=()):
    columns = weights.shape[1]
    rows = sum(part.shape[0] * part.shape[1] for part in parts)
    return call(
        functools.partial(first_kernel, len(parts), block),
        "first_sweep",
        [shape((rows, columns)), shape((copies, 1, rows))],
        [pltpu.VMEM((rows, weights.shape[0]), BF16), pltpu.VMEM((rows, LANES), F32)],
        after=after,
        flops=8 * rows * columns * weights.shape[0],
    )(*parts, weights)


def scale_rows(sum_refs, row_scale):
    scale = 1.0 / read_sums(sum_refs)
    row_scale[...] = jnp.broadcast_to(scale, (LANES, scale.shape[1])).T


def column_scale(plan, row_scale, start):
    weighted = plan[:, start : start + LANES] * row_scale[...]
    return 1.0 / jnp.sum(weighted, axis=0, keepdims=True)


def sweep_kernel(plan, *refs):
    sum_refs, (sums, _, row_scale, partial) = refs[:-4], refs[-4:]
    scale_rows(sum_refs, row_scale)
    for start in range(0, plan.shape[1], LANES):
        terms = plan[:, start : start + LANES] * column_scale(plan, row_scale, start)
        if start == 0:
            partial[...] = terms
        else:
            partial[...] += terms
    store_sums(sums, partial)


def sweep_call(plan, copies, row_sums):
    rows = plan.shape[0]
    return call(
        sweep_kernel,
        "sweep",
        [shape((copies, 1, rows)), shape(plan.shape)],
        [pltpu.VMEM((rows, LANES), F32)] * 2,
        aliases={0: 1},
    )(plan, *row_sums)


def total_kernel(rows, *refs):
    shares, share = refs[:-1], refs[-1]
    back, totals = decode_sum(shares, rows)
    store_code(share, back / totals, totals)


def total_call(shares, rows, after):
    out = shape(shares[0].shape, I16)
    return call(functools.partial(total_kernel, rows), "student_totals", out, after=after)(*shares)


def last_kernel(share, count, block, place, plan, unit_protos, *refs):
    sum_refs, refs = refs[:count], refs[count:]
    outs, (row_scale, scaled, mixed) = refs[:-3], refs[-3:]
    own = scaled.shape[0]
    width, columns = unit_protos.shape
    scale_rows(sum_refs, row_scale)
    for start in range(0, columns, block):
        here = slice(start, start + block)
        total = None
        for group in range(start, start + block, LANES):
            terms = plan[:own, group : group + LANES] * column_scale(plan, row_scale, group)
            total = terms if total is None else total + terms
            scaled[:, group - start : group - start + LANES] = terms.astype(BF16)
        sides = dot_t(scaled[...], unit_protos[:, here])
        if start == 0:
            mixed[:, width:] = total
            mixed[:, :width] = sides
        else:
            mixed[:, width:] += total
            mixed[:, :width] += sides
    for k, out in enumerate(outs):
        first = pl.multiple_of(jnp.bitwise_xor(place[0], k) * share, share)
        out[...] = mixed[pl.ds(first, share), :]


def last_call(place, plan, unit_protos, sums, own, count, block, after=()):
    rows = plan.shape[0]
    width = unit_protos.shape[0]
    share = own // count
    return call(
        functools.partial(last_kernel, share, len(sums), block),
        "last_sweep",
        [shape((share, width + LANES))] * count,
        [
            pltpu.VMEM((rows, LANES), F32),
            pltpu.VMEM((own, block), BF16),
            pltpu.VMEM((own, width + LANES), F32),
        ],
        scalars=1,
        after=after,
    )(place, plan, unit_protos, *sums)


def as_column(row):
    return jnp.broadcast_to(row, (LANES, row.shape[1])).T[:, :1]


def lane_sums(values):
    return jnp.sum(values, axis=1, keepdims=True)


def code_kernel(*refs):
    parts, out = refs[:-1], refs[-1]
    width = parts[0].shape[1] - LANES
    total = tree_sum([part[...] for part in parts])
    store_code(out, total[:, :width], lane_sums(total[:, width:]))


def code_call(parts, after=()):
    rows, columns = parts[0].shape
    out = coded(rows, columns - LANES)
    return call(code_kernel, "code_mixed", out, after=after)(*parts)


def mean_kernel(*refs):
    parts, out = refs[:-1], refs[-1]
    mixed, totals = decode_sum(parts, out.shape[0])
    out[...] = mixed / totals


def mean_call(parts, width, after=()):
    rows = (parts[0].shape[0] - ROW_TILE) * LANES // width
    return call(mean_kernel, "mean_protos", shape((rows, width)), after=after)(*parts)


FIELDS = 4


def prepare_kernel(place, feats, picked, weights, *refs):
    shares, (base, fields, expected, totals) = refs[:-4], refs[-4:]
    rows = expected.shape[0] // len(shares)
    for k, part in enumerate(shares):
        first = pl.multiple_of(jnp.bitwise_xor(place[0], k) * rows, rows)
        values, extra = decode(part, rows)
        expected[pl.ds(first, rows), :] = values
        totals[pl.ds(first, rows), :] = jnp.broadcast_to(extra, (rows, LANES))
    images = feats.shape[1]
    lane = lax.broadcasted_iota(jnp.int32, (images, LANES), 1)
    for crop in range(feats.shape[0]):
        here = slice(crop * images, (crop + 1) * images)
        raw = feats[crop].astype(F32)
        scales = lax.rsqrt(lane_sums(raw * raw) + epsilon)
        factor = as_column(weights[crop : crop + 1, :].astype(F32)) * (scales * (1.0 / student_softness))
        cubic = factor * scales * scales
        mean = expected[here, :]
        base[here, :] = factor * mean - (cubic * lane_sums(raw * mean)) * raw
        logs = jnp.log(totals[here, :])
        view = as_column(picked[crop : crop + 1, :].astype(F32))
        fields[here, :] = jnp.where(
            lane == 0, factor, jnp.where(lane == 1, cubic, jnp.where(lane == 2, scales, logs))
        )
        fields[here, :] = jnp.where(lane == FIELDS, view, fields[here, :])


def prepare_call(place, feats, picked, weights, shares, after=()):
    crops, images, width = feats.shape
    rows = crops * images
    return call(
        prepare_kernel,
        "prepare",
        [shape((rows, width)), shape((rows, LANES))],
        [pltpu.VMEM((rows, width), F32), pltpu.VMEM((rows, LANES), F32)],
        scalars=1,
        after=after,
    )(place, feats, picked, weights, *shares)


def finish_kernel(views, place, feats, base, fields, *refs):
    parts, (gradient, loss, means) = refs[:-3], refs[-3:]
    rows = parts[0].shape[0]
    for k, part in enumerate(parts):
        first = pl.multiple_of(jnp.bitwise_xor(place[0], k) * rows, rows)
        means[pl.ds(first, rows), :] = part[...]
    images = feats.shape[1]
    for crop in range(feats.shape[0]):
        here = slice(crop * images, (crop + 1) * images)
        raw = feats[crop].astype(F32)
        factor, cubic, scales = (fields[here, k : k + 1] for k in range(3))
        view_column = fields[here, FIELDS : FIELDS + 1]
        chosen = means[:images, :]
        for view in range(1, views):
            chosen = jnp.where(view_column == view, means[view * images : (view + 1) * images, :], chosen)
        along = cubic * lane_sums(raw * chosen)
        gradient[crop] = base[here, :] - factor * chosen + along * raw
        unit = (raw * scales).astype(BF16).astype(F32)
        column = fields[here, FIELDS - 1 : FIELDS] - lane_sums(unit * chosen) * (1.0 / student_softness)
        loss[crop : crop + 1, :] = jnp.broadcast_to(column, (images, LANES)).T[:1, :]


def finish_call(views, place, feats, base, fields, means):
    crops, images, width = feats.shape
    return call(
        functools.partial(finish_kernel, views),
        "finish",
        [shape((crops, images, width)), shape((crops, images))],
        [pltpu.VMEM((views * images, width), F32)],
        scalars=1,
    )(place, feats, base, fields, *means)


def shards(teacher_feats, student_feats, teacher_protos, student_protos, pairing, row_weight):
    images, views, width = teacher_feats.shape
    crops = student_feats.shape[0]
    image_devices = lax.axis_size("image")
    crop_devices = lax.axis_size("crop")
    proto_devices = lax.axis_size("proto")
    crop_place = lax.axis_index("crop").reshape(1)
    proto_place = lax.axis_index("proto").reshape(1)
    block = 1024

    teacher_parts = [teacher_feats] + [swap(teacher_feats, "image", k) for k in range(1, image_devices)]
    feats = student_feats.reshape(crops * images, width)
    protos = [student_protos] + [swap(student_protos, "crop", k) for k in range(1, crop_devices)]

    teacher_rows = image_devices * images * views
    joint = crops * images % (proto_devices * ROW_TILE) == 0 and 3 * teacher_rows == (ROW_TILE - SUMS_AT) * LANES
    pieces, copies = (proto_devices, 1) if joint else (1, crop_devices * proto_devices)
    if not joint:
        proto_place = jnp.zeros((1,), jnp.int32)

    def from_all(shares):
        return [shares[0]] + [swap(shares[k % len(shares)], "proto", k) for k in range(1, proto_devices)]

    def exchange(sums, shares):
        if joint:
            parts = [sums] + [swap(sums, "crop", k) for k in range(1, crop_devices)]
            return from_all(pack_call(parts, shares)), []
        return from_all(shares), [lax.all_to_all(sums, ("crop", "proto"), 0, 0)]

    unit_protos, unit_teacher, unit_feats, back = own_call(
        crop_place, proto_place, feats, student_protos, teacher_protos, block
    )
    half = student_protos.shape[1] // (2 * block) * block
    back = begin_call(unit_feats, back, protos[1:], half, block)
    plan, sums = first_call(teacher_parts, unit_teacher, copies, block, after=[back])
    shares = other_call(proto_place, unit_feats, back, protos[1:], pieces, half, block)
    for _ in range(SWEEPS - 2):
        shares, row_sums = exchange(sums, shares)
        sums, plan = sweep_call(plan, copies, row_sums or shares)
        shares = [total_call(shares, crops * images // pieces, [sums])]
    if joint:
        shares, row_sums = exchange(sums, shares)
    else:
        row_sums = [lax.all_to_all(sums, ("crop", "proto"), 0, 0)]
    mixed = last_call(
        crop_place, plan, unit_protos, row_sums or shares, views * images, crop_devices, block
    )

    sent = code_call([mixed[0]] + [swap(mixed[k], "crop", k) for k in range(1, crop_devices)])
    base, fields = prepare_call(proto_place, student_feats, pairing, row_weight, shares, after=[sent])
    means = mean_call(from_all([sent]), width, after=[base])
    means = [means] + [swap(means, "crop", k) for k in range(1, crop_devices)]
    return finish_call(views, crop_place, student_feats, base, fields, means)


def solution(mesh):
    in_specs = (
        P("image", None, None),
        P("crop", "image", None),
        P(None, ("crop", "proto")),
        P(None, ("crop", "proto")),
        P("crop", "image"),
        P("crop", "image"),
    )
    out_specs = (P("crop", "image", None), P("crop", "image"))
    return jax.shard_map(shards, mesh=mesh, in_specs=in_specs, out_specs=out_specs, check_vma=False)
```
